256 devices in a mesh: sub: 2 (over x_hi), row: 8 (over y, core), col: 16 (over x_lo, z).
Axes of the slice: x: 4 (x_hi: 2, x_lo: 2; x = x_hi * 2 + x_lo), y: 4, z: 8, core: 2. Of those that a mesh axis runs over, the one named last changes fastest.
Arguments:
- child_update: float32 [2, 4096, 4096], P('sub', 'row', 'col'), as said below
- child_coupling: bfloat16 [2, 4096, 2048], P('sub', 'row', 'col'), may hold values from -0.0625 to 0.0625
- pivot_inverse: bfloat16 [2, 2048, 2048], P('sub', 'col'), as said below
- child_map: int32 [2, 16], replicated, may hold values from 0 to 31, as said below
- parent_front: float32 [8192, 8192], P(('sub', 'row'), 'col'), as said below
- block_pattern: int32 [32, 32], P(('sub', 'row'), 'col'), may hold values from 0 to 1, as said below
Outputs:
- factored: float32 [8192, 8192], P(('sub', 'row'), 'col')
The draws below stay inside these ranges and needn't reach their ends.
Inputs may be any that keep to these rules, and one draw needn't show every extreme that they name: child_map[s, b] is the parent block that block b of child s lands in, for rows and columns alike; one child's values are distinct, and child_map[s, b] // 2 == b. `block_pattern`: Symmetric, with ones on the diagonal and in every block row and block column below 2. `child_update`: each child's matrix is symmetric. `parent_front`: Symmetric. `pivot_inverse`: each child's matrix is lower triangular with a nonzero diagonal.
All inputs are finite; a program needn't handle non-finite values.
Results may differ from the reference program's by a relative error of at most 0.0019.
Values may be sent and summed in bfloat16 or wider, within the bound.
A program may use at most 64 MiB of HBM per device.

```python
import math
import jax
import jax.numpy as jnp
from jax import lax

BLK = 256
KC = 2048
MC = 4096
FP = 8192
PSTEPS = 2
NBC = 16
NBP = 32
CB = 1
CBP = 2
KP = 512


def draw_child_update(key, part):
    noise_key, diag_key, basis_key = jax.random.split(jax.random.fold_in(key, 11), 3)
    basis_width = 2 * BLK
    noise_draw = jnp.clip(jax.random.normal(noise_key, (2, MC, MC), jnp.float32), -6.0, 6.0)
    basis_draw = jnp.clip(jax.random.normal(basis_key, (2, MC, basis_width), jnp.float32), -6.0, 6.0)
    diagonal = jax.random.uniform(diag_key, (2, MC), jnp.float32, 3.0, 4.0)
    symmetric = (noise_draw + jnp.swapaxes(noise_draw, 1, 2)) * (0.05 / math.sqrt(2.0 * MC))
    scaled_basis = basis_draw * math.sqrt(3.0 / basis_width)
    gram_part = jnp.einsum('smr,snr->smn', scaled_basis, scaled_basis, precision=lax.Precision.HIGHEST)
    diag_index = jnp.arange(MC)
    return (gram_part + symmetric).at[:, diag_index, diag_index].add(diagonal)


def draw_pivot_inverse(key, part):
    noise_key, diag_key = jax.random.split(jax.random.fold_in(key, 23))
    noise_draw = jnp.clip(jax.random.normal(noise_key, (2, KC, KC), jnp.float32), -6.0, 6.0)
    diagonal = jax.random.uniform(diag_key, (2, KC), jnp.float32, 0.8, 1.25)
    strict_lower = jnp.tril(noise_draw, -1) * (1.0 / math.sqrt(KC))
    diag_index = jnp.arange(KC)
    return strict_lower.at[:, diag_index, diag_index].set(diagonal).astype(jnp.bfloat16)


def pin_first(ordering, value):
    swapped = jnp.where(ordering == value, ordering[0], ordering)
    return swapped.at[0].set(value)


def draw_child_map(key, part):
    groups = NBC // CB
    key_list = jax.random.split(jax.random.fold_in(key, 37), 2 * groups)
    orders = jax.vmap(lambda subkey: jax.random.permutation(subkey, CBP))(key_list)
    orders = orders.at[0].set(pin_first(orders[0], 0))
    orders = orders.at[2 * groups - 1].set(pin_first(orders[2 * groups - 1], CBP - 1))
    offsets = jnp.arange(2 * groups, dtype=jnp.int32) % groups * CBP
    return (orders[:, :CB] + offsets[:, None]).reshape(2, NBC).astype(jnp.int32)


def draw_parent_front(key, part):
    noise_key, diag_key = jax.random.split(jax.random.fold_in(key, 41))
    noise_draw = jnp.clip(jax.random.normal(noise_key, (FP, FP), jnp.float32), -6.0, 6.0)
    diagonal = jax.random.uniform(diag_key, (FP,), jnp.float32, 1.0, 1.5)
    symmetric = (noise_draw + noise_draw.T) * (1.0 / math.sqrt(2.0 * FP))
    diag_index = jnp.arange(FP)
    return symmetric.at[diag_index, diag_index].add(diagonal)


def draw_block_pattern(key, part):
    bits_draw = jax.random.randint(jax.random.fold_in(key, 53), (NBP, NBP), 0, 2, jnp.int32)
    strict_lower = jnp.tril(bits_draw, -1)
    pattern = strict_lower + strict_lower.T + jnp.eye(NBP, dtype=jnp.int32)
    leading = jnp.arange(NBP, dtype=jnp.int32) < PSTEPS
    dense_part = leading[:, None] | leading[None, :]
    return jnp.where(dense_part, jnp.int32(1), pattern).astype(jnp.int32)


def steps_of(key, dims, shards, least, top_value):
    factor_of = 1.0
    for position, parts in shards:
        heights = jax.random.uniform(jax.random.fold_in(jax.random.fold_in(key, 6), position), (parts,), jnp.float32, least / len(shards), top_value / len(shards))
        factor_of = factor_of * jnp.repeat(jnp.exp(heights), dims[position] // parts).reshape((-1,) + (1,) * (len(dims) - 1 - position))
    return factor_of


def noise(stream_key, extent, deviation, limit, cuts=(), kind=jnp.bfloat16):
    values = deviation * jax.random.normal(stream_key, extent, jnp.float32)
    if cuts:
        values = values * steps_of(stream_key, extent, cuts, -0.22, 0.18)
    return jnp.clip(values, -limit, limit).astype(kind)


def setup_inputs(seed: int = 0) -> dict:
    arg_keys = jax.random.split(jax.random.key(seed), 7)
    child_update = draw_child_update(jax.random.fold_in(arg_keys[6], 71), 0)
    child_coupling = noise(arg_keys[1], (2, MC, KC), (4 * KC) ** -0.5, 0.0625, ((0, 2), (1, 8), (2, 16)))
    pivot_inverse = draw_pivot_inverse(jax.random.fold_in(arg_keys[6], 71), 0)
    child_map = draw_child_map(jax.random.fold_in(arg_keys[6], 71), 0)
    parent_front = draw_parent_front(jax.random.fold_in(arg_keys[6], 71), 0)
    block_pattern = draw_block_pattern(jax.random.fold_in(arg_keys[6], 71), 0)
    return {"child_update": child_update, "child_coupling": child_coupling, "pivot_inverse": pivot_inverse, "child_map": child_map, "parent_front": parent_front, "block_pattern": block_pattern}


def reference(child_update, child_coupling, pivot_inverse, child_map, parent_front, block_pattern):
    pattern = block_pattern.astype(jnp.float32)
    assembled = parent_front.reshape(NBP, BLK, NBP, BLK) * pattern[:, None, :, None]
    for child_index in range(2):
        child_panel = jnp.dot(child_coupling[child_index].astype(jnp.float32), pivot_inverse[child_index].T.astype(jnp.float32), preferred_element_type=jnp.float32).astype(jnp.bfloat16)
        schur_part = child_update[child_index] - jnp.dot(child_panel.astype(jnp.float32), child_panel.T.astype(jnp.float32), preferred_element_type=jnp.float32)
        blocks = schur_part.reshape(NBC, BLK, NBC, BLK).transpose(0, 2, 1, 3)
        mapping = child_map[child_index]
        assembled = assembled.at[mapping[:, None], :, mapping[None, :], :].add(blocks)
    assembled = assembled.reshape(FP, FP)
    identity = jnp.eye(BLK, dtype=jnp.float32)
    for step_index in range(PSTEPS):
        edge_low = step_index * BLK
        edge_high = edge_low + BLK
        lower_pivot = jnp.linalg.cholesky(assembled[edge_low:edge_high, edge_low:edge_high])
        inverse = jax.scipy.linalg.solve_triangular(lower_pivot, identity, lower=True)
        below_rows = jnp.dot(assembled[edge_high:, edge_low:edge_high], inverse.T, precision=lax.Precision.HIGHEST)
        assembled = assembled.at[edge_high:, edge_high:].add(-jnp.dot(below_rows, below_rows.T, precision=lax.Precision.HIGHEST))
        assembled = assembled.at[edge_low:edge_high, edge_low:edge_high].set(lower_pivot)
        assembled = assembled.at[edge_high:, edge_low:edge_high].set(below_rows)
    row_ids = jnp.arange(FP, dtype=jnp.int32)[:, None]
    col_ids = jnp.arange(FP, dtype=jnp.int32)[None, :]
    return jnp.where((row_ids < KP) & (col_ids > row_ids), jnp.float32(0.0), assembled)
```

```python
import jax
import jax.numpy as jnp
from jax import lax
from jax.experimental import pallas as pl
from jax.experimental.pallas import tpu as pltpu
from jax.sharding import PartitionSpec as P

f32 = jnp.float32
bf16 = jnp.bfloat16
MESH = pl.DeviceIdType.MESH
NT = (((1,), (1,)), ((), ()))
NN = (((1,), (0,)), ((), ()))
TN = (((0,), (0,)), ((), ()))


def rcopy(src, dst, send, recv, dev):
    return pltpu.make_async_remote_copy(
        src_ref=src, dst_ref=dst, send_sem=send, recv_sem=recv, device_id=dev, device_id_type=MESH
    )


class Ring:
    def __init__(self, buf, send, recv, s, r, xlo, z):
        self.right, self.left = [], []
        to_right = (s, r, xlo * 8 + lax.rem(z + 1, 8))
        to_left = (s, r, xlo * 8 + lax.rem(z + 7, 8))
        for t in range(4):
            slot = buf.at[lax.rem(z - t + 8, 8)]
            self.right.append(rcopy(slot, slot, send.at[t], recv.at[t], to_right))
        for t in range(3):
            slot = buf.at[lax.rem(z + t, 8)]
            self.left.append(rcopy(slot, slot, send.at[4 + t], recv.at[4 + t], to_left))

    def start(self, t):
        self.right[t].start()
        if t < 3:
            self.left[t].start()

    def arrive(self, t):
        self.right[t].wait_recv()
        if t < 3:
            self.left[t].wait_recv()

    def drain(self):
        for copy in self.right + self.left:
            copy.wait_send()


class Column:
    def __init__(self, buf, send, recv, s, r, c):
        core = lax.rem(r, 2)
        h = 4 * s + r // 2
        own = buf.at[8 * s + r]
        partner = (s, r + 1 - 2 * core, c)
        self.out, self.share = [], [rcopy(own, own, send.at[7], recv.at[7], partner)]
        for d in range(1, 8):
            to = lax.rem(h + d, 8)
            dev = (to // 4, 2 * lax.rem(to, 4) + core, c)
            self.out.append(rcopy(own, own, send.at[d - 1], recv.at[d - 1], dev))
            slot = buf.at[2 * lax.rem(h - d + 8, 8) + core]
            self.share.append(rcopy(slot, slot, send.at[7 + d], recv.at[7 + d], partner))

    def start(self):
        for copy in self.out:
            copy.start()
        self.share[0].start()

    def forward(self, d):
        self.out[d - 1].wait_recv()
        self.share[d].start()

    def finish(self):
        for copy in self.share:
            copy.wait_recv()

    def drain(self):
        for copy in self.out + self.share:
            copy.wait_send()


def gather_kernel(
    map_ref, pat_ref, upd_ref, cpl_ref, inv_ref, front_ref,
    a_ref, ag_ref, col_ref,
    invbuf, cbuf, ptile, prow, pcol, ubuf, f00, a00,
    loc_sem, x_send, x_recv, u_send, u_recv,
    c_send, c_recv, p_send, p_recv, f_send, f_recv, g_send, g_recv,
    pr_send, pr_recv, pc_send, pc_recv, k1_send, k1_recv, k2_send, k2_recv,
    fs_send, fs_recv, cs_send, cs_recv, as_send, as_recv,
):
    s, r, c = lax.axis_index("sub"), lax.axis_index("row"), lax.axis_index("col")
    xlo, z = c // 8, lax.rem(c, 8)
    group = 8 * s + r
    lead = group == 0
    root = jnp.logical_and(lead, c == 0)
    xpart = (s, r, lax.rem(c + 8, 16))

    inv_loc = pltpu.make_async_copy(inv_ref.at[0], invbuf.at[xlo], loc_sem.at[0])
    inv_rem = rcopy(inv_ref.at[0], invbuf.at[xlo], x_send.at[0], x_recv.at[0], xpart)
    mine = pl.ds(pl.multiple_of(xlo * 256, 256), 256)
    theirs = pl.ds(pl.multiple_of(256 - xlo * 256, 256), 256)
    cpl_loc = pltpu.make_async_copy(cpl_ref.at[0, mine], cbuf.at[z, xlo], loc_sem.at[1])
    cpl_rem = rcopy(cpl_ref.at[0, theirs], cbuf.at[z, xlo], x_send.at[1], x_recv.at[1], xpart)
    cpl_rem.start()
    cpl_loc.start()
    inv_loc.start()
    inv_rem.start()
    u_copies = []
    for i in range(2):
        block = 2 * r + i
        dest = (block // 8, lax.rem(block, 8), c)
        src = upd_ref.at[0, pl.ds(256 * i, 256)]
        rem = rcopy(src, ubuf.at[s], u_send.at[i], u_recv.at[s], dest)
        loc = pltpu.make_async_copy(src, ubuf.at[s], u_recv.at[s])
        own = jnp.logical_and(block // 8 == s, lax.rem(block, 8) == r)
        u_copies.append((own, rem))

        @pl.when(own)
        def _():
            loc.start()

        @pl.when(jnp.logical_not(own))
        def _():
            rem.start()

    cpl_loc.wait()
    cpl_rem.wait_recv()
    ring_c = Ring(cbuf, c_send, c_recv, s, r, xlo, z)
    ring_c.start(0)

    def weight(child, i, k):
        ro = map_ref[child, group] - 2 * group
        co = map_ref[child, c] - 2 * c
        return (ro == i).astype(f32) * (co == k).astype(f32)

    for child in range(2):
        rcopy(ubuf.at[child], ubuf.at[child], u_send.at[0], u_recv.at[child], xpart).wait_recv()
    for i in range(2):
        for k in range(2):
            at = (slice(256 * i, 256 * i + 256), slice(256 * k, 256 * k + 256))
            value = front_ref[at] * pat_ref[i, k].astype(f32)
            for child in range(2):
                value = value + weight(child, i, k) * ubuf[child]
            a_ref[at] = value

    fs_copies = []
    for cp in range(16):
        piece = a_ref.at[pl.ds(64 * (cp % 8), 64)]
        fs_copies.append(rcopy(piece, f00.at[cp % 8], fs_send.at[cp], fs_recv.at[0], (0, 0, cp)))

    @pl.when(root)
    def _():
        pltpu.make_async_copy(a_ref.at[pl.ds(0, 64)], f00.at[0], fs_recv.at[0]).start()
        for copy in fs_copies[1:]:
            copy.start()

    for t in range(1, 4):
        ring_c.arrive(t - 1)
        ring_c.start(t)
    ring_f = Ring(f00, f_send, f_recv, s, r, xlo, z)

    @pl.when(lead)
    def _():
        rcopy(f00.at[0], f00.at[0], fs_send.at[0], fs_recv.at[0], xpart).wait_recv()
        ring_f.start(0)

    inv_loc.wait()
    inv_rem.wait_recv()
    ring_c.arrive(3)

    for half in range(2):
        total = jnp.zeros((256, 128), f32)
        for kz in range(8):
            for kh in range(2):
                total = total + lax.dot_general(
                    cbuf[kz, kh],
                    invbuf[half, :, (kh * 8 + kz) * 128 : (kh * 8 + kz + 1) * 128],
                    NT,
                    preferred_element_type=f32,
                )
        ptile[:, 128 * half : 128 * half + 128] = total.astype(bf16)

    block = 2 * r + xlo
    pr_copies = []
    for xh in range(2):
        dest = (block // 8, lax.rem(block, 8), xh * 8 + z)
        rem = rcopy(ptile, prow.at[z, s], pr_send.at[xh], pr_recv.at[s], dest)
        loc = pltpu.make_async_copy(ptile, prow.at[z, s], pr_recv.at[s])
        own = jnp.logical_and(
            jnp.logical_and(block // 8 == s, lax.rem(block, 8) == r), xlo == xh
        )
        pr_copies.append((own, rem))

        @pl.when(own)
        def _():
            loc.start()

        @pl.when(jnp.logical_not(own))
        def _():
            rem.start()

    pc_slot = pcol.at[2 * z + s]
    pc_rem = rcopy(
        ptile, pc_slot, pc_send.at[0], pc_recv.at[0], (z // 4, 2 * lax.rem(z, 4) + s, block)
    )
    pc_loc = pltpu.make_async_copy(ptile, pc_slot, pc_recv.at[0])
    pc_own = jnp.logical_and(
        jnp.logical_and(z // 4 == s, 2 * lax.rem(z, 4) + s == r), block == c
    )

    @pl.when(pc_own)
    def _():
        pc_loc.start()

    @pl.when(jnp.logical_not(pc_own))
    def _():
        pc_rem.start()

    for child in range(2):
        slot = prow.at[z, child]
        rcopy(slot, slot, pr_send.at[0], pr_recv.at[child], xpart).wait_recv()
    ring_p = Ring(prow, p_send, p_recv, s, r, xlo, z)
    ring_p.start(0)
    rcopy(pcol.at[group], pcol.at[group], pc_send.at[0], pc_recv.at[0], xpart).wait_recv()
    col_p = Column(pcol, k1_send, k1_recv, s, r, c)
    col_p.start()
    for t in range(1, 4):
        ring_p.arrive(t - 1)
        ring_p.start(t)

        @pl.when(lead)
        def _():
            ring_f.arrive(t - 1)
            ring_f.start(t)

        col_p.forward(2 * t - 1)
        col_p.forward(2 * t)
    col_p.forward(7)
    ring_p.arrive(3)
    col_p.finish()

    def product(child, columns):
        total = jnp.zeros((256, 256), f32)
        for kz in range(8):
            total = total + lax.dot_general(
                prow[kz, child], columns(kz, child), NT, preferred_element_type=f32
            )
        return total

    @pl.when(root)
    def _():
        for copy in fs_copies[1:]:
            copy.wait_send()

    schur = [product(child, lambda kz, ch: pcol[2 * kz + ch]) for child in range(2)]
    for i in range(2):
        for k in range(2):
            at = (slice(256 * i, 256 * i + 256), slice(256 * k, 256 * k + 256))
            a_ref[at] = a_ref[at] - weight(0, i, k) * schur[0] - weight(1, i, k) * schur[1]

    as_copies, cs_copies = [], []
    for cp in range(16):
        as_copies.append(
            rcopy(
                a_ref.at[pl.ds(64 * (cp % 8), 64)], ag_ref.at[cp % 8],
                as_send.at[cp], as_recv.at[0], (c // 8, lax.rem(c, 8), cp),
            )
        )
        source = a_ref if cp % 2 else a00
        cs_copies.append(
            rcopy(
                source.at[pl.ds(64 * (cp // 2), 64)], col_ref.at[cp],
                cs_send.at[cp], cs_recv.at[0], (cp // 8, cp % 8, c),
            )
        )

    @pl.when(lead)
    def _():
        ring_f.arrive(3)
        ring_f.drain()
        lead_prod = [product(child, lambda kz, ch: prow[kz, ch]) for child in range(2)]
        for i in range(2):
            for k in range(2):
                for q in range(4):
                    value = f00[4 * i + q, :, 256 * k : 256 * k + 256]
                    for child in range(2):
                        off = map_ref[child, 0]
                        w = (off == i).astype(f32) * (off == k).astype(f32)
                        value = value - w * lead_prod[child][64 * q : 64 * q + 64]
                    a00[256 * i + 64 * q : 256 * i + 64 * q + 64, 256 * k : 256 * k + 256] = value
        pltpu.make_async_copy(a00.at[pl.ds(0, 64)], col_ref.at[0], cs_recv.at[0]).start()
        for copy in cs_copies[1:]:
            copy.start()

        @pl.when(c == 0)
        def _():
            pltpu.make_async_copy(a_ref.at[pl.ds(0, 64)], ag_ref.at[0], as_recv.at[0]).start()

        @pl.when(c != 0)
        def _():
            as_copies[0].start()

        for copy in as_copies[1:]:
            copy.start()

    rcopy(col_ref.at[group], col_ref.at[group], cs_send.at[0], cs_recv.at[0], xpart).wait_recv()
    col_a = Column(col_ref, k2_send, k2_recv, s, r, c)
    col_a.start()
    rcopy(ag_ref.at[z], ag_ref.at[z], as_send.at[0], as_recv.at[0], xpart).wait_recv()
    ring_g = Ring(ag_ref, g_send, g_recv, s, r, xlo, z)
    ring_g.start(0)
    for t in range(1, 4):
        ring_g.arrive(t - 1)
        ring_g.start(t)
        col_a.forward(2 * t - 1)
        col_a.forward(2 * t)
    col_a.forward(7)
    ring_g.arrive(3)
    col_a.finish()

    @pl.when(lead)
    def _():
        for copy in cs_copies[1:] + as_copies[1:]:
            copy.wait_send()

        @pl.when(c != 0)
        def _():
            as_copies[0].wait_send()

    for own, rem in u_copies + pr_copies + [(pc_own, pc_rem)]:
        @pl.when(jnp.logical_not(own))
        def _():
            rem.wait_send()

    cpl_rem.wait_send()
    inv_rem.wait_send()
    for ring in (ring_c, ring_p, ring_g, col_p, col_a):
        ring.drain()


def gather_call(child_map, pattern, update, coupling, inverse, front):
    vmem = pl.BlockSpec(memory_space=pltpu.VMEM)
    smem = pl.BlockSpec(memory_space=pltpu.SMEM)
    dma = pltpu.SemaphoreType.DMA
    ring = [dma((7,)), dma((7,))]
    column = [dma((15,)), dma((15,))]
    return pl.pallas_call(
        gather_kernel,
        out_shape=[
            jax.ShapeDtypeStruct((512, 512), f32),
            jax.ShapeDtypeStruct((8, 64, 512), f32),
            jax.ShapeDtypeStruct((16, 64, 512), f32),
        ],
        in_specs=[smem, smem, vmem, vmem, vmem, vmem],
        out_specs=[vmem, vmem, vmem],
        scratch_shapes=[
            pltpu.VMEM((2, 128, 2048), bf16),
            pltpu.VMEM((8, 2, 256, 128), bf16),
            pltpu.VMEM((256, 256), bf16),
            pltpu.VMEM((8, 2, 256, 256), bf16),
            pltpu.VMEM((16, 256, 256), bf16),
            pltpu.VMEM((2, 256, 256), f32),
            pltpu.VMEM((8, 64, 512), f32),
            pltpu.VMEM((512, 512), f32),
            dma((2,)), dma((2,)), dma((2,)), dma((2,)), dma((2,)),
            *ring, *ring, *ring, *ring,
            dma((2,)), dma((2,)), dma((1,)), dma((1,)),
            *column, *column,
            dma((16,)), dma((1,)), dma((16,)), dma((1,)), dma((16,)), dma((1,)),
        ],
        compiler_params=pltpu.CompilerParams(
            has_side_effects=True, vmem_limit_bytes=48 * 1024 * 1024
        ),
        cost_estimate=pl.CostEstimate(flops=800_000_000, bytes_accessed=8_000_000, transcendentals=0),
    )(child_map, pattern, update, coupling, inverse, front)


def lanes(x, k):
    return jnp.broadcast_to(x[:, k : k + 1], (8, 128))


def rows(x, k):
    return jnp.broadcast_to(x[k : k + 1, :], (8, 128))


def pivot_block(d):
    left = [d[8 * i : 8 * i + 8, :] for i in range(16)]
    rid = lax.broadcasted_iota(jnp.int32, (8, 128), 0)
    cid = lax.broadcasted_iota(jnp.int32, (8, 128), 1)
    right = [(cid == rid + 8 * i).astype(f32) for i in range(16)]
    for b in range(16):
        lead = [lanes(left[b], 8 * b + k) for k in range(8)]
        lo, ro = left[b], right[b]
        top, inv, row_l, row_r = {}, [], [], []
        for k in range(8):
            rinv = lax.rsqrt(rows(lead[k], k))
            f = jnp.where(rid > k, lead[k] * rinv, 0.0)
            for m in range(k + 1, 8):
                top[k, m] = rows(lead[m], k) * rinv
                lead[m] = lead[m] - f * top[k, m]
            row_l.append(rows(lo, k) * rinv)
            row_r.append(rows(ro, k) * rinv)
            lo = lo - f * row_l[k]
            ro = ro - f * row_r[k]
            inv.append(rinv)
        left[b], right[b] = row_l[0], row_r[0]
        for k in range(1, 8):
            left[b] = jnp.where(rid == k, row_l[k], left[b])
            right[b] = jnp.where(rid == k, row_r[k], right[b])
        for i in range(b + 1, 16):
            own = [lanes(left[i], 8 * b + k) for k in range(8)]
            lo, ro = left[i], right[i]
            for k in range(8):
                f = own[k] * inv[k]
                for m in range(k + 1, 8):
                    own[m] = own[m] - f * top[k, m]
                lo = lo - f * row_l[k]
                ro = ro - f * row_r[k]
            left[i], right[i] = lo, ro
    return left, right


def hdot(a, b, dims):
    return lax.dot_general(a, b, dims, precision=lax.Precision.HIGHEST, preferred_element_type=f32)


def factor_kernel(a_ref, ag_ref, col_ref, o_ref, lead, both, ut, vt):
    s, r, c = lax.axis_index("sub"), lax.axis_index("row"), lax.axis_index("col")
    group = 8 * s + r
    for h in range(8):
        lead[64 * h : 64 * h + 64, :] = col_ref[2 * h]
        both[64 * h : 64 * h + 64, 0:512] = ag_ref[h]
        both[64 * h : 64 * h + 64, 512:1024] = col_ref[2 * h + 1]

    @pl.loop(0, 4)
    def _(kb):
        at = pl.ds(pl.multiple_of(kb * 128, 128), 128)
        left, right = pivot_block(lead[at, at])
        for i in range(16):
            ut[8 * i : 8 * i + 8, :] = left[i]
            vt[8 * i : 8 * i + 8, :] = right[i]
        row_id = lax.broadcasted_iota(jnp.int32, (512, 128), 0)
        panel = hdot(lead[:, at], vt[...], NT)
        panel = jnp.where(row_id >= (kb + 1) * 128, panel, 0.0)
        lead[...] = lead[...] - hdot(panel, panel, NT)
        done = hdot(vt[...], both[at, :], NN)
        both[...] = both[...] - hdot(panel, done, NN)
        both[at, :] = done
        lead[:, at] = panel
        lead[at, at] = ut[...].T

    row_id = lax.broadcasted_iota(jnp.int32, (512, 512), 0)
    col_id = lax.broadcasted_iota(jnp.int32, (512, 512), 1)

    @pl.when(group == 0)
    def _():
        keep = jnp.logical_and(c == 0, col_id <= row_id)
        o_ref[...] = jnp.where(keep, lead[...], 0.0)

    @pl.when(jnp.logical_and(group != 0, c == 0))
    def _():
        o_ref[...] = both[:, 0:512].T

    @pl.when(jnp.logical_and(group != 0, c != 0))
    def _():
        o_ref[...] = a_ref[...] - hdot(both[:, 0:512], both[:, 512:1024], TN)


def factor_call(tile, row_part, col_part):
    vmem = pl.BlockSpec(memory_space=pltpu.VMEM)
    return pl.pallas_call(
        factor_kernel,
        out_shape=jax.ShapeDtypeStruct((512, 512), f32),
        in_specs=[vmem, vmem, vmem],
        out_specs=vmem,
        scratch_shapes=[
            pltpu.VMEM((512, 512), f32),
            pltpu.VMEM((512, 1024), f32),
            pltpu.VMEM((128, 128), f32),
            pltpu.VMEM((128, 128), f32),
        ],
        compiler_params=pltpu.CompilerParams(vmem_limit_bytes=48 * 1024 * 1024),
        cost_estimate=pl.CostEstimate(flops=5_000_000_000, bytes_accessed=5_000_000, transcendentals=512),
    )(tile, row_part, col_part)


def local(child_update, child_coupling, pivot_inverse, child_map, parent_front, block_pattern):
    tile, row_part, col_part = gather_call(
        child_map, block_pattern, child_update, child_coupling, pivot_inverse, parent_front
    )
    return factor_call(tile, row_part, col_part)


def solution(mesh):
    return jax.shard_map(
        local,
        mesh=mesh,
        in_specs=(
            P("sub", "row", "col"),
            P("sub", "row", "col"),
            P("sub", "col", None),
            P(),
            P(("sub", "row"), "col"),
            P(("sub", "row"), "col"),
        ),
        out_specs=P(("sub", "row"), "col"),
        check_vma=False,
    )
```

```python
import jax
import jax.numpy as jnp
from jax import lax
from jax.experimental import pallas as pl
from jax.experimental.pallas import tpu as pltpu
from jax.sharding import PartitionSpec as P

f32 = jnp.float32
bf16 = jnp.bfloat16
MESH = pl.DeviceIdType.MESH
NT = (((1,), (1,)), ((), ()))
NN = (((1,), (0,)), ((), ()))
TN = (((0,), (0,)), ((), ()))


def rcopy(src, dst, send, recv, dev):
    return pltpu.make_async_remote_copy(
        src_ref=src, dst_ref=dst, send_sem=send, recv_sem=recv, device_id=dev, device_id_type=MESH
    )


def aligned(start, size):
    return pl.ds(pl.multiple_of(start, size), size)


class Ring:
    def __init__(self, buf, send, recv, s, r, xlo, z):
        self.buf, self.send, self.recv, self.z = buf, send, recv, z
        self.to_right = (s, r, xlo * 8 + lax.rem(z + 1, 8))
        self.to_left = (s, r, xlo * 8 + lax.rem(z + 7, 8))

    def right(self, t):
        slot = self.buf.at[lax.rem(self.z - t + 8, 8)]
        return rcopy(slot, slot, self.send.at[t], self.recv.at[t], self.to_right)

    def left(self, t):
        slot = self.buf.at[lax.rem(self.z + t, 8)]
        return rcopy(slot, slot, self.send.at[4 + t], self.recv.at[4 + t], self.to_left)

    def both(self, t, act):
        act(self.right(t))
        if isinstance(t, int):
            if t < 3:
                act(self.left(t))
        else:

            @pl.when(t < 3)
            def _():
                act(self.left(t))

    def start(self, t):
        self.both(t, lambda copy: copy.start())

    def arrive(self, t):
        self.both(t, lambda copy: copy.wait_recv())

    def drain(self):
        for t in range(4):
            self.both(t, lambda copy: copy.wait_send())


class Spread:
    def __init__(self, slot, send, recv, n, chip, core, device, partner):
        self.slot, self.send, self.recv, self.n = slot, send, recv, n
        self.chip, self.core, self.device, self.partner = chip, core, device, partner

    def out(self, d):
        own = self.slot(2 * self.chip + self.core)
        to = lax.rem(self.chip + d, self.n)
        return rcopy(own, own, self.send.at[d], self.recv.at[d], self.device(to))

    def share(self, d):
        slot = self.slot(2 * lax.rem(self.chip - d + self.n, self.n) + self.core)
        return rcopy(slot, slot, self.send.at[self.n + d], self.recv.at[self.n + d], self.partner)

    def start(self):
        for d in range(1, self.n):
            self.out(d).start()
        self.share(0).start()

    def forward(self, d):
        self.out(d).wait_recv()
        self.share(d).start()

    def finish(self):
        for d in range(self.n):
            self.share(d).wait_recv()

    def drain(self):
        for d in range(1, self.n):
            self.out(d).wait_send()
        for d in range(self.n):
            self.share(d).wait_send()


def lanes(x, k):
    return jnp.broadcast_to(x[:, k : k + 1], (8, 128))


def rows(x, k):
    return jnp.broadcast_to(x[k : k + 1, :], (8, 128))


def pivot_block(d):
    left = [d[8 * i : 8 * i + 8, :] for i in range(16)]
    rid = lax.broadcasted_iota(jnp.int32, (8, 128), 0)
    cid = lax.broadcasted_iota(jnp.int32, (8, 128), 1)
    right = [(cid == rid + 8 * i).astype(f32) for i in range(16)]
    for b in range(16):
        lead = [lanes(left[b], 8 * b + k) for k in range(8)]
        lo, ro = left[b], right[b]
        top, inv, row_l, row_r = {}, [], [], []
        for k in range(8):
            rinv = lax.rsqrt(rows(lead[k], k))
            f = jnp.where(rid > k, lead[k] * rinv, 0.0)
            for m in range(k + 1, 8):
                top[k, m] = rows(lead[m], k) * rinv
                lead[m] = lead[m] - f * top[k, m]
            row_l.append(rows(lo, k) * rinv)
            row_r.append(rows(ro, k) * rinv)
            lo = lo - f * row_l[k]
            ro = ro - f * row_r[k]
            inv.append(rinv)
        left[b], right[b] = row_l[0], row_r[0]
        for k in range(1, 8):
            left[b] = jnp.where(rid == k, row_l[k], left[b])
            right[b] = jnp.where(rid == k, row_r[k], right[b])
        for i in range(b + 1, 16):
            own = [lanes(left[i], 8 * b + k) for k in range(8)]
            lo, ro = left[i], right[i]
            for k in range(8):
                f = own[k] * inv[k]
                for m in range(k + 1, 8):
                    own[m] = own[m] - f * top[k, m]
                lo = lo - f * row_l[k]
                ro = ro - f * row_r[k]
            left[i], right[i] = lo, ro
    return left, right


def hdot(a, b, dims):
    return lax.dot_general(a, b, dims, precision=lax.Precision.HIGHEST, preferred_element_type=f32)


def kernel(
    map_ref, pat_ref, upd_ref, cpl_ref, inv_ref, front_ref, o_ref,
    invbuf, cbuf, ptile, prow, pcol, ubuf, front, tile, fsrc, fbuf, gbuf,
    fc, p0, tbuf, lead, both, ut, vt,
    loc_sem, fa_send, fa_recv, fb_send, fb_recv, d1_send, d1_recv, d2_send, d2_recv,
    t_send, t_recv, x_send, x_recv, u_send, u_recv, c_send, c_recv, p_send, p_recv,
    g_send, g_recv, pr_send, pr_recv, pc_send, pc_recv, k1_send, k1_recv, kf_send, kf_recv,
    rs_send, rs_recv, rp_send, rp_recv, gs_send, gs_recv, cs_send, cs_recv, e_send, e_recv,
):
    s, r, c = lax.axis_index("sub"), lax.axis_index("row"), lax.axis_index("col")
    xlo, z = c // 8, lax.rem(c, 8)
    y, core = r // 2, lax.rem(r, 2)
    group = 8 * s + r
    chip = 4 * s + y
    leads = group == 0
    root = jnp.logical_and(leads, c == 0)
    block = 2 * r + xlo
    xpart = (s, r, lax.rem(c + 8, 16))
    cpart = (s, r + 1 - 2 * core, c)
    hpart = (1 - s, r, c)

    def at_group(g):
        return (g // 8, lax.rem(g, 8), c)

    inv_loc = pltpu.make_async_copy(inv_ref.at[0], invbuf.at[xlo], loc_sem.at[0])
    mine, theirs = aligned(xlo * 256, 256), aligned(256 - xlo * 256, 256)
    cpl_loc = pltpu.make_async_copy(cpl_ref.at[0, mine], cbuf.at[z, xlo], loc_sem.at[1])
    front_loc = pltpu.make_async_copy(front_ref, front, loc_sem.at[2])
    inv_loc.start()
    cpl_loc.start()
    front_loc.start()

    barrier = pltpu.get_barrier_semaphore()

    def same(dev):
        return jnp.logical_and(jnp.logical_and(dev[0] == s, dev[1] == r), dev[2] == c)

    def hello(dev):
        pl.semaphore_signal(barrier, inc=1, device_id=dev, device_id_type=MESH)

    def hello_other(dev):
        @pl.when(jnp.logical_not(same(dev)))
        def _():
            hello(dev)

    for d in range(1, 16):
        hello((s, r, lax.rem(c + d, 16)))
        hello(at_group(lax.rem(group + d, 16)))
    half_block = group // 2
    for child in range(2):
        hello_other((child, half_block, lax.rem(group, 2) * 8 + z))
    hello_other((core, c // 2, lax.rem(c, 2) * 8 + chip))
    hello_other((0, 0, group))
    pr_dest = [(block // 8, lax.rem(block, 8), xh * 8 + z) for xh in range(2)]
    pc_dest = (z // 4, 2 * lax.rem(z, 4) + s, block)

    def other(dev):
        return jnp.where(same(dev), 0, 1)

    expected = 30 + other(pr_dest[0]) + other(pr_dest[1]) + other(pc_dest)
    expected = expected + jnp.where(leads, 16 - jnp.where(c == 0, 1, 0), 0)
    pl.semaphore_wait(barrier, expected)

    fa_copies = [
        rcopy(cpl_ref.at[0, pl.ds(32 * q, 32)], fc.at[c], fa_send.at[q], fa_recv.at[0], (s, q, c))
        for q in range(1, 8)
    ]
    u_copies = []
    for i in range(2):
        dest = at_group(2 * r + i)
        u_copies.append((same(dest), rcopy(
            upd_ref.at[0, pl.ds(256 * i, 256)], ubuf.at[s], u_send.at[i], u_recv.at[s], dest
        ), i))

    def u_start(entry):
        own, rem, i = entry

        @pl.when(own)
        def _():
            pltpu.make_async_copy(
                upd_ref.at[0, pl.ds(256 * i, 256)], ubuf.at[s], u_recv.at[s]
            ).start()

        @pl.when(jnp.logical_not(own))
        def _():
            rem.start()

    @pl.when(r == 0)
    def _():
        for copy in fa_copies:
            copy.start()
        pltpu.make_async_copy(cpl_ref.at[0, pl.ds(0, 32)], fc.at[c], fa_recv.at[0]).start()
        u_start(u_copies[0])

    cpl_rem = rcopy(cpl_ref.at[0, theirs], cbuf.at[z, xlo], x_send.at[1], x_recv.at[1], xpart)
    cpl_rem.start()
    inv_half = aligned(64 * core, 64)
    inv_rem = rcopy(
        inv_ref.at[0, inv_half], invbuf.at[xlo, inv_half], x_send.at[0], x_recv.at[0], xpart
    )
    inv_rem.start()

    rcopy(fc.at[c], fc.at[c], fa_send.at[0], fa_recv.at[0], xpart).wait_recv()
    fb_copies = [
        rcopy(fc.at[c], fc.at[c], fb_send.at[d], fb_recv.at[d], (s, r, lax.rem(c + d, 16)))
        for d in range(1, 16)
    ]
    for copy in fb_copies:
        copy.start()

    cpl_loc.wait()
    cpl_rem.wait_recv()
    ring_c = Ring(cbuf, c_send, c_recv, s, r, xlo, z)
    ring_c.start(0)

    def weight(child, i, k):
        ro = map_ref[child, group] - 2 * group
        co = map_ref[child, c] - 2 * c
        return (ro == i).astype(f32) * (co == k).astype(f32)

    def quarter(i, k):
        return (slice(256 * i, 256 * i + 256), slice(256 * k, 256 * k + 256))

    def own_entries():
        for child in range(2):
            slot = ubuf.at[child]
            rcopy(slot, slot, u_send.at[0], u_recv.at[child], xpart).wait_recv()
        for i in range(2):
            for k in range(2):
                value = front[quarter(i, k)] * pat_ref[i, k].astype(f32)
                for child in range(2):
                    value = value + weight(child, i, k) * ubuf[child]
                tile[quarter(i, k)] = value

    front_loc.wait()
    gs_copies, cs_copies, rs_copies = [], [], []
    for cp in range(16):
        gs_copies.append(rcopy(
            fsrc.at[pl.ds(64 * (cp % 8), 64)], gbuf.at[cp % 8],
            gs_send.at[cp], gs_recv.at[0], (c // 8, lax.rem(c, 8), cp),
        ))
        piece = fsrc.at[pl.ds(32 * cp, 32)]
        cs_copies.append(rcopy(
            piece, fbuf.at[cp, 1], cs_send.at[cp], cs_recv.at[0], (cp // 8, cp % 8, c)
        ))
        rs_copies.append(rcopy(
            piece, fbuf.at[cp, 0], rs_send.at[cp], rs_recv.at[0], (cp // 8, cp % 8, 0)
        ))

    @pl.when(leads)
    def _():
        own_entries()
        fsrc[...] = tile[...].astype(bf16)

        @pl.when(c == 0)
        def _():
            for copy in rs_copies[1:]:
                copy.start()
            pltpu.make_async_copy(fsrc.at[pl.ds(0, 32)], fbuf.at[0, 0], rs_recv.at[0]).start()
            pltpu.make_async_copy(fsrc.at[pl.ds(0, 64)], gbuf.at[0], gs_recv.at[0]).start()

        pltpu.make_async_copy(fsrc.at[pl.ds(0, 32)], fbuf.at[0, 1], cs_recv.at[0]).start()
        for copy in cs_copies[1:]:
            copy.start()

        @pl.when(c != 0)
        def _():
            gs_copies[0].start()

        for copy in gs_copies[1:]:
            copy.start()

    for copy in fb_copies:
        copy.wait_recv()
    inv_loc.wait()
    wide = jnp.concatenate([fc[i] for i in range(16)], axis=1)
    piece = lax.dot_general(wide, invbuf[xlo], NT, preferred_element_type=f32).astype(bf16)
    my_rows = aligned(32 * r, 32)
    p0[s, z, my_rows, aligned(128 * xlo, 128)] = piece
    d1_copies = []
    for d in range(1, 16):
        slot = p0.at[s, z, my_rows, aligned(128 * xlo, 128)]
        d1_copies.append(rcopy(
            slot, slot, d1_send.at[d], d1_recv.at[d], (s, r, lax.rem(c + d, 16))
        ))
    for copy in d1_copies:
        copy.start()

    inv_rem.wait_recv()
    other_half = invbuf.at[1 - xlo, inv_half]
    inv_share = rcopy(other_half, other_half, x_send.at[2], x_recv.at[2], cpart)
    inv_share.start()
    ring_c.arrive(0)
    ring_c.start(1)

    rp_copies = [
        rcopy(fbuf.at[group, 0], fbuf.at[group, 0], rp_send.at[d], rp_recv.at[0], (s, r, d))
        for d in range(16)
    ]

    @pl.when(c == 0)
    def _():
        slot = fbuf.at[group, 0]
        rcopy(slot, slot, rs_send.at[0], rs_recv.at[0], xpart).wait_recv()
        for copy in rp_copies[1:]:
            copy.start()

    for copy in d1_copies:
        copy.wait_recv()
    spread_0 = Spread(
        lambda q: p0.at[s, :, aligned(32 * q, 32), :], d2_send, d2_recv, 4, y, core,
        lambda to: (s, 2 * to + core, c), cpart,
    )
    spread_0.start()
    ring_c.arrive(1)
    ring_c.start(2)
    for d in range(1, 4):
        spread_0.forward(d)
    ring_c.arrive(2)
    ring_c.start(3)

    slot = fbuf.at[group, 1]
    rcopy(slot, slot, cs_send.at[0], cs_recv.at[0], xpart).wait_recv()

    @pl.when(c != 0)
    def _():
        rp_copies[0].wait_recv()

    spread_f = Spread(
        lambda q: fbuf.at[q], kf_send, kf_recv, 8, chip, core,
        lambda to: at_group(2 * to + core), cpart,
    )
    spread_f.start()
    spread_0.finish()

    def product(left, right):
        total = jnp.zeros((256, 256), f32)
        for kz in range(8):
            total = total + lax.dot_general(
                left(kz), right(kz), NT, preferred_element_type=f32
            )
        return total

    tbuf[s] = product(lambda kz: p0[s, kz], lambda kz: p0[s, kz])
    t_parts = [tbuf.at[s, pl.ds(128, 128)], tbuf.at[s, pl.ds(0, 128), pl.ds(0, 128)]]
    t_copies = [rcopy(t_parts[i], t_parts[i], t_send.at[i], t_recv.at[i], hpart) for i in range(2)]
    for copy in t_copies:
        copy.start()

    inv_share.wait_recv()
    ring_c.arrive(3)
    for half in range(2):
        total = jnp.zeros((256, 128), f32)
        for kz in range(8):
            for kh in range(2):
                total = total + lax.dot_general(
                    cbuf[kz, kh],
                    invbuf[half, :, (kh * 8 + kz) * 128 : (kh * 8 + kz + 1) * 128],
                    NT,
                    preferred_element_type=f32,
                )
        ptile[:, 128 * half : 128 * half + 128] = total.astype(bf16)

    own_copies = []
    for xh in range(2):
        slot = prow.at[z, s]
        own_copies.append((
            same(pr_dest[xh]), rcopy(ptile, slot, pr_send.at[xh], pr_recv.at[s], pr_dest[xh]),
            slot, pr_recv.at[s],
        ))
    slot = pcol.at[2 * z + s]
    own_copies.append((
        same(pc_dest), rcopy(ptile, slot, pc_send.at[0], pc_recv.at[0], pc_dest),
        slot, pc_recv.at[0],
    ))
    for own, rem, slot, sem in own_copies:
        @pl.when(own)
        def _():
            pltpu.make_async_copy(ptile, slot, sem).start()

        @pl.when(jnp.logical_not(own))
        def _():
            rem.start()

    for d in range(1, 8):
        spread_f.forward(d)

    for child in range(2):
        slot = prow.at[z, child]
        rcopy(slot, slot, pr_send.at[0], pr_recv.at[child], xpart).wait_recv()
    ring_p = Ring(prow, p_send, p_recv, s, r, xlo, z)
    ring_p.start(0)
    rcopy(pcol.at[group], pcol.at[group], pc_send.at[0], pc_recv.at[0], xpart).wait_recv()
    spread_p = Spread(
        lambda q: pcol.at[q], k1_send, k1_recv, 8, chip, core,
        lambda to: at_group(2 * to + core), cpart,
    )
    spread_p.start()
    spread_f.finish()
    for copy in t_copies:
        copy.wait()

    @pl.when(r != 0)
    def _():
        u_start(u_copies[0])

    u_start(u_copies[1])
    p0_half = aligned(4 * core, 4)
    e_half = rcopy(p0.at[s, p0_half], p0.at[s, p0_half], e_send.at[0], e_recv.at[0], hpart)
    e_half.start()
    e_got = p0.at[1 - s, p0_half]
    e_share = rcopy(e_got, e_got, e_send.at[1], e_recv.at[1], cpart)
    ring_g = Ring(gbuf, g_send, g_recv, s, r, xlo, z)
    rcopy(gbuf.at[z], gbuf.at[z], gs_send.at[0], gs_recv.at[0], xpart).wait_recv()
    ring_g.start(0)

    @pl.when(root)
    def _():
        lead[...] = tile[...]

    @pl.when(jnp.logical_not(root))
    def _():
        for q in range(16):
            lead[32 * q : 32 * q + 32, :] = fbuf[q, 0].astype(f32)

    for child in range(2):
        for i in range(2):
            w = (map_ref[child, 0] == i).astype(f32)
            o = 256 * i
            at = (slice(o, o + 128), slice(o, o + 128))
            lead[at] = lead[at] - w * tbuf[child, 0:128, 0:128]
            at = (slice(o + 128, o + 256), slice(o, o + 256))
            lead[at] = lead[at] - w * tbuf[child, 128:256, :]

    @pl.loop(0, 4)
    def _(kb):
        at = aligned(kb * 128, 128)
        left, right = pivot_block(lead[at, at])
        for i in range(16):
            ut[8 * i : 8 * i + 8, :] = left[i]
            vt[kb, 8 * i : 8 * i + 8, :] = right[i]
        ring_p.arrive(kb)
        ring_g.arrive(kb)

        @pl.when(kb < 3)
        def _():
            ring_p.start(kb + 1)
            ring_g.start(kb + 1)
            spread_p.forward(2 * kb + 1)
            spread_p.forward(2 * kb + 2)

        @pl.when(kb == 3)
        def _():
            spread_p.forward(7)

        @pl.when(kb == 1)
        def _():
            e_half.wait_recv()
            e_share.start()

        row_id = lax.broadcasted_iota(jnp.int32, (512, 128), 0)
        panel = hdot(lead[:, at], vt[kb], NT)
        panel = jnp.where(row_id >= (kb + 1) * 128, panel, 0.0)
        lead[...] = lead[...] - hdot(panel, panel, NT)
        lead[:, at] = panel
        lead[at, at] = ut[...].T

    spread_p.finish()
    e_share.wait_recv()

    @pl.when(jnp.logical_not(leads))
    def _():
        own_entries()

    for h in range(8):
        both[64 * h : 64 * h + 64, 0:512] = gbuf[h].astype(f32)
        both[64 * h : 64 * h + 32, 512:1024] = fbuf[2 * h, 1].astype(f32)
        both[64 * h + 32 : 64 * h + 64, 512:1024] = fbuf[2 * h + 1, 1].astype(f32)
    for child in range(2):
        schur = product(lambda kz: prow[kz, child], lambda kz: pcol[2 * kz + child])
        row_part = product(lambda kz: p0[child, kz], lambda kz: prow[kz, child])
        col_part = product(lambda kz: p0[child, kz], lambda kz: pcol[2 * kz + child])
        lo = map_ref[child, 0]
        ro = map_ref[child, group] - 2 * group
        co = map_ref[child, c] - 2 * c
        for i in range(2):
            w = (lo == i).astype(f32)
            for k in range(2):
                tile[quarter(i, k)] = tile[quarter(i, k)] - weight(child, i, k) * schur
                at = quarter(i, k)
                both[at] = both[at] - w * (ro == k).astype(f32) * row_part
                at = quarter(i, k + 2)
                both[at] = both[at] - w * (co == k).astype(f32) * col_part

    @pl.when(c == 0)
    def _():
        both[:, 0:512] = tile[...].T

    for kb in range(4):
        at = slice(128 * kb, 128 * kb + 128)
        done = hdot(vt[kb], both[at, :], NN)
        both[at, :] = done
        if kb < 3:
            below = slice(128 * kb + 128, 512)
            both[below, :] = both[below, :] - hdot(lead[below, at], done, NN)

    @pl.when(leads)
    def _():
        row_id = lax.broadcasted_iota(jnp.int32, (512, 512), 0)
        col_id = lax.broadcasted_iota(jnp.int32, (512, 512), 1)
        keep = jnp.logical_and(c == 0, col_id <= row_id)
        o_ref[...] = jnp.where(keep, lead[...], 0.0)

    @pl.when(jnp.logical_and(jnp.logical_not(leads), c == 0))
    def _():
        o_ref[...] = both[:, 0:512].T

    @pl.when(jnp.logical_and(jnp.logical_not(leads), c != 0))
    def _():
        o_ref[...] = tile[...] - hdot(both[:, 0:512], both[:, 512:1024], TN)

    @pl.when(r == 0)
    def _():
        for copy in fa_copies:
            copy.wait_send()

    @pl.when(root)
    def _():
        for copy in rs_copies[1:]:
            copy.wait_send()

    @pl.when(leads)
    def _():
        for copy in cs_copies[1:] + gs_copies[1:]:
            copy.wait_send()

        @pl.when(c != 0)
        def _():
            gs_copies[0].wait_send()

    @pl.when(c == 0)
    def _():
        for copy in rp_copies[1:]:
            copy.wait_send()

    for entry in u_copies + own_copies:
        @pl.when(jnp.logical_not(entry[0]))
        def _():
            entry[1].wait_send()

    for copy in fb_copies + d1_copies + [cpl_rem, inv_rem, inv_share, e_half, e_share]:
        copy.wait_send()
    for gather in (ring_c, ring_p, ring_g, spread_0, spread_f, spread_p):
        gather.drain()


def local(child_update, child_coupling, pivot_inverse, child_map, parent_front, block_pattern):
    vmem = pl.BlockSpec(memory_space=pltpu.VMEM)
    smem = pl.BlockSpec(memory_space=pltpu.SMEM)
    hbm = pl.BlockSpec(memory_space=pl.ANY)
    dma = pltpu.SemaphoreType.DMA

    def pair(n, m):
        return [dma((n,)), dma((m,))]

    return pl.pallas_call(
        kernel,
        out_shape=jax.ShapeDtypeStruct((512, 512), f32),
        in_specs=[smem, smem, hbm, hbm, hbm, hbm],
        out_specs=vmem,
        scratch_shapes=[
            pltpu.VMEM((2, 128, 2048), bf16),
            pltpu.VMEM((8, 2, 256, 128), bf16),
            pltpu.VMEM((256, 256), bf16),
            pltpu.VMEM((8, 2, 256, 256), bf16),
            pltpu.VMEM((16, 256, 256), bf16),
            pltpu.VMEM((2, 256, 256), f32),
            pltpu.VMEM((512, 512), f32),
            pltpu.VMEM((512, 512), f32),
            pltpu.VMEM((512, 512), bf16),
            pltpu.VMEM((16, 2, 32, 512), bf16),
            pltpu.VMEM((8, 64, 512), bf16),
            pltpu.VMEM((16, 32, 128), bf16),
            pltpu.VMEM((2, 8, 256, 256), bf16),
            pltpu.VMEM((2, 256, 256), f32),
            pltpu.VMEM((512, 512), f32),
            pltpu.VMEM((512, 1024), f32),
            pltpu.VMEM((128, 128), f32),
            pltpu.VMEM((4, 128, 128), f32),
            dma((3,)), *pair(8, 1), *pair(16, 16), *pair(16, 16), *pair(8, 8),
            *pair(2, 2), *pair(3, 3), *pair(2, 2), *pair(7, 7), *pair(7, 7),
            *pair(7, 7), *pair(2, 2), *pair(1, 1), *pair(16, 16), *pair(16, 16),
            *pair(16, 1), *pair(16, 1), *pair(16, 1), *pair(16, 1), *pair(2, 2),
        ],
        compiler_params=pltpu.CompilerParams(
            has_side_effects=True, collective_id=0, vmem_limit_bytes=60 * 1024 * 1024
        ),
        cost_estimate=pl.CostEstimate(
            flops=8_000_000_000, bytes_accessed=4_000_000, transcendentals=512
        ),
    )(child_map, block_pattern, child_update, child_coupling, pivot_inverse, parent_front)


def solution(mesh):
    return jax.shard_map(
        local,
        mesh=mesh,
        in_specs=(
            P("sub", "row", "col"),
            P("sub", "row", "col"),
            P("sub", "col", None),
            P(),
            P(("sub", "row"), "col"),
            P(("sub", "row"), "col"),
        ),
        out_specs=P(("sub", "row"), "col"),
        check_vma=False,
    )
```

```python
import jax
import jax.numpy as jnp
from jax import lax
from jax.experimental import pallas as pl
from jax.experimental.pallas import tpu as pltpu
from jax.sharding import PartitionSpec as P

f32 = jnp.float32
bf16 = jnp.bfloat16
MESH = pl.DeviceIdType.MESH
NT = (((1,), (1,)), ((), ()))
NN = (((1,), (0,)), ((), ()))
TN = (((0,), (0,)), ((), ()))


def rcopy(src, dst, send, recv, dev):
    return pltpu.make_async_remote_copy(
        src_ref=src, dst_ref=dst, send_sem=send, recv_sem=recv, device_id=dev, device_id_type=MESH
    )


def aligned(start, size):
    return pl.ds(pl.multiple_of(start, size), size)


class Ring:
    def __init__(self, slot, send, recv, right_last, s, r, xlo, z):
        self.slot, self.send, self.recv, self.z = slot, send, recv, z
        self.right_last = right_last
        self.to_right = (s, r, xlo * 8 + lax.rem(z + 1, 8))
        self.to_left = (s, r, xlo * 8 + lax.rem(z + 7, 8))

    def right(self, t):
        slot = self.slot(lax.rem(self.z - t + 8, 8))
        return rcopy(slot, slot, self.send.at[t], self.recv.at[t], self.to_right)

    def left(self, t):
        slot = self.slot(lax.rem(self.z + t, 8))
        return rcopy(slot, slot, self.send.at[4 + t], self.recv.at[4 + t], self.to_left)

    def both(self, t, act):
        long, short = (self.right, self.left) if self.right_last else (self.left, self.right)
        act(long(t))
        if isinstance(t, int):
            if t < 3:
                act(short(t))
        else:

            @pl.when(t < 3)
            def _():
                act(short(t))

    def start(self, t):
        self.both(t, lambda copy: copy.start())

    def arrive(self, t):
        self.both(t, lambda copy: copy.wait_recv())

    def step(self, t):
        self.arrive(t)
        if isinstance(t, int):
            if t < 3:
                self.start(t + 1)
        else:

            @pl.when(t < 3)
            def _():
                self.start(t + 1)

    def drain(self):
        for t in range(4):
            self.both(t, lambda copy: copy.wait_send())


class Spread:
    def __init__(self, slot, send, recv, n, chip, core, device, partner):
        self.slot, self.send, self.recv, self.n = slot, send, recv, n
        self.chip, self.core, self.device, self.partner = chip, core, device, partner

    def out(self, d):
        own = self.slot(2 * self.chip + self.core)
        to = lax.rem(self.chip + d, self.n)
        return rcopy(own, own, self.send.at[d], self.recv.at[d], self.device(to))

    def share(self, d):
        slot = self.slot(2 * lax.rem(self.chip - d + self.n, self.n) + self.core)
        return rcopy(slot, slot, self.send.at[self.n + d], self.recv.at[self.n + d], self.partner)

    def start(self):
        for d in range(1, self.n):
            self.out(d).start()
        self.share(0).start()

    def forward(self, d):
        self.out(d).wait_recv()
        self.share(d).start()

    def finish(self):
        for d in range(self.n):
            self.share(d).wait_recv()

    def drain(self):
        for d in range(1, self.n):
            self.out(d).wait_send()
        for d in range(self.n):
            self.share(d).wait_send()


def lanes(x, k):
    return jnp.broadcast_to(x[:, k : k + 1], (8, 128))


def rows(x, k):
    return jnp.broadcast_to(x[k : k + 1, :], (8, 128))


def pivot_block(d, hook):
    left = [d[8 * i : 8 * i + 8, :] for i in range(16)]
    rid = lax.broadcasted_iota(jnp.int32, (8, 128), 0)
    cid = lax.broadcasted_iota(jnp.int32, (8, 128), 1)
    right = [(cid == rid + 8 * i).astype(f32) for i in range(16)]
    for b in range(16):
        lead = [lanes(left[b], 8 * b + k) for k in range(8)]
        lo, ro = left[b], right[b]
        top, inv, row_l, row_r = {}, [], [], []
        for k in range(8):
            rinv = lax.rsqrt(rows(lead[k], k))
            f = jnp.where(rid > k, lead[k] * rinv, 0.0)
            for m in range(k + 1, 8):
                top[k, m] = rows(lead[m], k) * rinv
                lead[m] = lead[m] - f * top[k, m]
            row_l.append(rows(lo, k) * rinv)
            row_r.append(rows(ro, k) * rinv)
            lo = lo - f * row_l[k]
            ro = ro - f * row_r[k]
            inv.append(rinv)
        left[b], right[b] = row_l[0], row_r[0]
        for k in range(1, 8):
            left[b] = jnp.where(rid == k, row_l[k], left[b])
            right[b] = jnp.where(rid == k, row_r[k], right[b])
        for i in range(b + 1, 16):
            own = [lanes(left[i], 8 * b + k) for k in range(8)]
            lo, ro = left[i], right[i]
            for k in range(8):
                f = own[k] * inv[k]
                for m in range(k + 1, 8):
                    own[m] = own[m] - f * top[k, m]
                lo = lo - f * row_l[k]
                ro = ro - f * row_r[k]
            left[i], right[i] = lo, ro
        if b == 5:
            hook()
    return left, right


def halves(x):
    high = x.astype(bf16)
    return high, (x - high.astype(f32)).astype(bf16)


def hdot(a, b, dims):
    (ah, al), (bh, bl) = halves(a), halves(b)

    def part(x, y):
        return lax.dot_general(x, y, dims, preferred_element_type=f32)

    return part(ah, bh) + (part(ah, bl) + part(al, bh))


def kernel(
    map_ref, pat_ref, upd_ref, cpl_ref, inv_ref, front_ref, o_ref,
    invbuf, cbuf, ptile, prow, pcol, ubuf, front, tile, fsrc, fbuf, gbuf,
    fc, p0, tbuf, lead, both, ut, vt,
    loc_sem, fa_send, fa_recv, fb_send, fb_recv, d1_send, d1_recv, d2_send, d2_recv,
    t_send, t_recv, x_send, x_recv, u_send, u_recv, c_send, c_recv, p_send, p_recv,
    g_send, g_recv, pr_send, pr_recv, pc_send, pc_recv, k1_send, k1_recv, kf_send, kf_recv,
    rs_send, rs_recv, rp_send, rp_recv, gs_send, gs_recv, cs_send, cs_recv, e_send, e_recv,
):
    s, r, c = lax.axis_index("sub"), lax.axis_index("row"), lax.axis_index("col")
    xlo, z = c // 8, lax.rem(c, 8)
    y, core = r // 2, lax.rem(r, 2)
    group = 8 * s + r
    chip = 4 * s + y
    leads = group == 0
    root = jnp.logical_and(leads, c == 0)
    block = 2 * r + xlo
    xpart = (s, r, lax.rem(c + 8, 16))
    cpart = (s, r + 1 - 2 * core, c)
    hpart = (1 - s, r, c)

    def at_group(g):
        return (g // 8, lax.rem(g, 8), c)

    inv_loc = pltpu.make_async_copy(inv_ref.at[0], invbuf.at[xlo], loc_sem.at[0])
    mine, theirs = aligned(xlo * 256, 256), aligned(256 - xlo * 256, 256)
    cpl_loc = pltpu.make_async_copy(cpl_ref.at[0, mine], cbuf.at[z, xlo], loc_sem.at[1])
    front_loc = pltpu.make_async_copy(front_ref, front, loc_sem.at[2])
    inv_loc.start()
    cpl_loc.start()
    front_loc.start()

    barrier = pltpu.get_barrier_semaphore()

    def same(dev):
        return jnp.logical_and(jnp.logical_and(dev[0] == s, dev[1] == r), dev[2] == c)

    def hello(dev):
        pl.semaphore_signal(barrier, inc=1, device_id=dev, device_id_type=MESH)

    def hello_other(dev):
        @pl.when(jnp.logical_not(same(dev)))
        def _():
            hello(dev)

    for d in range(1, 16):
        hello((s, r, lax.rem(c + d, 16)))
        hello(at_group(lax.rem(group + d, 16)))
    half_block = group // 2
    for child in range(2):
        hello_other((child, half_block, lax.rem(group, 2) * 8 + z))
    hello_other((core, c // 2, lax.rem(c, 2) * 8 + chip))
    hello_other((0, 0, group))
    pr_dest = [(block // 8, lax.rem(block, 8), xh * 8 + z) for xh in range(2)]
    pc_dest = (z // 4, 2 * lax.rem(z, 4) + s, block)

    def other(dev):
        return jnp.where(same(dev), 0, 1)

    expected = 30 + other(pr_dest[0]) + other(pr_dest[1]) + other(pc_dest)
    expected = expected + jnp.where(leads, 16 - jnp.where(c == 0, 1, 0), 0)
    pl.semaphore_wait(barrier, expected)

    fa_copies = [
        rcopy(cpl_ref.at[0, pl.ds(32 * q, 32)], fc.at[c], fa_send.at[q], fa_recv.at[0], (s, q, c))
        for q in range(1, 8)
    ]
    u_copies = []
    for i in range(2):
        dest = at_group(2 * r + i)
        u_copies.append((same(dest), rcopy(
            upd_ref.at[0, pl.ds(256 * i, 256)], ubuf.at[s], u_send.at[i], u_recv.at[s], dest
        ), i))

    def u_start(entry):
        own, rem, i = entry

        @pl.when(own)
        def _():
            pltpu.make_async_copy(
                upd_ref.at[0, pl.ds(256 * i, 256)], ubuf.at[s], u_recv.at[s]
            ).start()

        @pl.when(jnp.logical_not(own))
        def _():
            rem.start()

    @pl.when(r == 0)
    def _():
        for copy in fa_copies:
            copy.start()
        pltpu.make_async_copy(cpl_ref.at[0, pl.ds(0, 32)], fc.at[c], fa_recv.at[0]).start()
        u_start(u_copies[0])

    cpl_rem = rcopy(cpl_ref.at[0, theirs], cbuf.at[z, xlo], x_send.at[1], x_recv.at[1], xpart)
    cpl_rem.start()
    inv_half = aligned(64 * core, 64)
    inv_rem = rcopy(
        inv_ref.at[0, inv_half], invbuf.at[xlo, inv_half], x_send.at[0], x_recv.at[0], xpart
    )
    inv_rem.start()

    rcopy(fc.at[c], fc.at[c], fa_send.at[0], fa_recv.at[0], xpart).wait_recv()
    fb_copies = [
        rcopy(fc.at[c], fc.at[c], fb_send.at[d], fb_recv.at[d], (s, r, lax.rem(c + d, 16)))
        for d in range(1, 16)
    ]
    for copy in fb_copies:
        copy.start()

    cpl_loc.wait()
    cpl_rem.wait_recv()
    ring_c = [
        Ring(lambda q, kh=kh: cbuf.at[q, kh], c_send.at[kh], c_recv.at[kh], kh == 0, s, r, xlo, z)
        for kh in range(2)
    ]
    for ring in ring_c:
        ring.start(0)

    @pl.when(r != 0)
    def _():
        u_start(u_copies[0])

    u_start(u_copies[1])
    for ring in ring_c:
        ring.step(0)

    def weight(child, i, k):
        ro = map_ref[child, group] - 2 * group
        co = map_ref[child, c] - 2 * c
        return (ro == i).astype(f32) * (co == k).astype(f32)

    def quarter(i, k):
        return (slice(256 * i, 256 * i + 256), slice(256 * k, 256 * k + 256))

    def own_entries():
        for child in range(2):
            slot = ubuf.at[child]
            rcopy(slot, slot, u_send.at[0], u_recv.at[child], xpart).wait_recv()
        for i in range(2):
            for k in range(2):
                value = front[quarter(i, k)] * pat_ref[i, k].astype(f32)
                for child in range(2):
                    value = value + weight(child, i, k) * ubuf[child]
                tile[quarter(i, k)] = value

    front_loc.wait()
    gs_copies, cs_copies, rs_copies = [], [], []
    for cp in range(16):
        gs_copies.append(rcopy(
            fsrc.at[pl.ds(64 * (cp % 8), 64)], gbuf.at[cp % 8],
            gs_send.at[cp], gs_recv.at[0], (c // 8, lax.rem(c, 8), cp),
        ))
        piece = fsrc.at[pl.ds(32 * cp, 32)]
        cs_copies.append(rcopy(
            piece, fbuf.at[cp, 1], cs_send.at[cp], cs_recv.at[0], (cp // 8, cp % 8, c)
        ))
        rs_copies.append(rcopy(
            piece, fbuf.at[cp, 0], rs_send.at[cp], rs_recv.at[0], (cp // 8, cp % 8, 0)
        ))

    for copy in fb_copies:
        copy.wait_recv()
    inv_loc.wait()
    wide = jnp.concatenate([fc[i] for i in range(16)], axis=1)
    piece = lax.dot_general(wide, invbuf[xlo], NT, preferred_element_type=f32).astype(bf16)
    my_rows = aligned(32 * r, 32)
    p0[s, z, my_rows, aligned(128 * xlo, 128)] = piece
    d1_copies = []
    for d in range(1, 16):
        slot = p0.at[s, z, my_rows, aligned(128 * xlo, 128)]
        d1_copies.append(rcopy(
            slot, slot, d1_send.at[d], d1_recv.at[d], (s, r, lax.rem(c + d, 16))
        ))
    for copy in d1_copies:
        copy.start()

    for ring in ring_c:
        ring.step(1)
    inv_rem.wait_recv()
    other_half = invbuf.at[1 - xlo, inv_half]
    inv_share = rcopy(other_half, other_half, x_send.at[2], x_recv.at[2], cpart)
    inv_share.start()

    @pl.when(leads)
    def _():
        own_entries()
        fsrc[...] = tile[...].astype(bf16)

        @pl.when(c == 0)
        def _():
            for copy in rs_copies[1:]:
                copy.start()
            pltpu.make_async_copy(fsrc.at[pl.ds(0, 32)], fbuf.at[0, 0], rs_recv.at[0]).start()
            pltpu.make_async_copy(fsrc.at[pl.ds(0, 64)], gbuf.at[0], gs_recv.at[0]).start()

        pltpu.make_async_copy(fsrc.at[pl.ds(0, 32)], fbuf.at[0, 1], cs_recv.at[0]).start()
        for copy in cs_copies[1:]:
            copy.start()

        @pl.when(c != 0)
        def _():
            gs_copies[0].start()

        for copy in gs_copies[1:]:
            copy.start()

    for ring in ring_c:
        ring.step(2)
    for copy in d1_copies:
        copy.wait_recv()
    spread_0 = Spread(
        lambda q: p0.at[s, :, aligned(32 * q, 32), :], d2_send, d2_recv, 4, y, core,
        lambda to: (s, 2 * to + core, c), cpart,
    )
    spread_0.start()

    rp_copies = [
        rcopy(fbuf.at[group, 0], fbuf.at[group, 0], rp_send.at[d], rp_recv.at[0], (s, r, d))
        for d in range(16)
    ]

    @pl.when(c == 0)
    def _():
        slot = fbuf.at[group, 0]
        rcopy(slot, slot, rs_send.at[0], rs_recv.at[0], xpart).wait_recv()
        for copy in rp_copies[1:]:
            copy.start()

    inv_share.wait_recv()
    for ring in ring_c:
        ring.step(3)
    wide = jnp.concatenate([cbuf[q % 8, q // 8] for q in range(16)], axis=1)
    for half in range(2):
        total = lax.dot_general(wide, invbuf[half], NT, preferred_element_type=f32)
        ptile[:, 128 * half : 128 * half + 128] = total.astype(bf16)

    own_copies = []
    for xh in range(2):
        slot = prow.at[z, s]
        own_copies.append((
            same(pr_dest[xh]), rcopy(ptile, slot, pr_send.at[xh], pr_recv.at[s], pr_dest[xh]),
            slot, pr_recv.at[s],
        ))
    slot = pcol.at[2 * z + s]
    own_copies.append((
        same(pc_dest), rcopy(ptile, slot, pc_send.at[0], pc_recv.at[0], pc_dest),
        slot, pc_recv.at[0],
    ))
    for own, rem, slot, sem in own_copies:
        @pl.when(own)
        def _():
            pltpu.make_async_copy(ptile, slot, sem).start()

        @pl.when(jnp.logical_not(own))
        def _():
            rem.start()

    for d in range(1, 4):
        spread_0.forward(d)

    for child in range(2):
        slot = prow.at[z, child]
        rcopy(slot, slot, pr_send.at[0], pr_recv.at[child], xpart).wait_recv()
    ring_p = [
        Ring(
            lambda q, child=child: prow.at[q, child],
            p_send.at[child], p_recv.at[child], child == 0, s, r, xlo, z,
        )
        for child in range(2)
    ]
    for ring in ring_p:
        ring.start(0)
    spread_0.finish()

    def across(left, right):
        return lax.dot_general(left, right, NT, preferred_element_type=f32)

    def panel_0(child):
        return jnp.concatenate([p0[child, kz] for kz in range(8)], axis=1)

    wide = panel_0(s)
    tbuf[s] = across(wide, wide)
    t_parts = [tbuf.at[s, pl.ds(128, 128)], tbuf.at[s, pl.ds(0, 128), pl.ds(0, 128)]]
    t_copies = [rcopy(t_parts[i], t_parts[i], t_send.at[i], t_recv.at[i], hpart) for i in range(2)]
    for copy in t_copies:
        copy.start()

    slot = fbuf.at[group, 1]
    rcopy(slot, slot, cs_send.at[0], cs_recv.at[0], xpart).wait_recv()

    @pl.when(c != 0)
    def _():
        rp_copies[0].wait_recv()

    spread_f = Spread(
        lambda q: fbuf.at[q], kf_send, kf_recv, 8, chip, core,
        lambda to: at_group(2 * to + core), cpart,
    )
    spread_f.start()
    rcopy(pcol.at[group], pcol.at[group], pc_send.at[0], pc_recv.at[0], xpart).wait_recv()
    spread_p = Spread(
        lambda q: pcol.at[q], k1_send, k1_recv, 8, chip, core,
        lambda to: at_group(2 * to + core), cpart,
    )
    spread_p.start()
    p0_half = aligned(4 * core, 4)
    e_half = rcopy(p0.at[s, p0_half], p0.at[s, p0_half], e_send.at[0], e_recv.at[0], hpart)
    e_half.start()
    e_got = p0.at[1 - s, p0_half]
    e_share = rcopy(e_got, e_got, e_send.at[1], e_recv.at[1], cpart)
    ring_g = Ring(lambda q: gbuf.at[q], g_send, g_recv, True, s, r, xlo, z)
    rcopy(gbuf.at[z], gbuf.at[z], gs_send.at[0], gs_recv.at[0], xpart).wait_recv()
    ring_g.start(0)
    for d in range(1, 8):
        spread_f.forward(d)
    spread_f.finish()
    for copy in t_copies:
        copy.wait()

    @pl.when(root)
    def _():
        lead[...] = tile[...]

    @pl.when(jnp.logical_not(root))
    def _():
        for q in range(16):
            lead[32 * q : 32 * q + 32, :] = fbuf[q, 0].astype(f32)

    for child in range(2):
        for i in range(2):
            w = (map_ref[child, 0] == i).astype(f32)
            o = 256 * i
            at = (slice(o, o + 128), slice(o, o + 128))
            lead[at] = lead[at] - w * tbuf[child, 0:128, 0:128]
            at = (slice(o + 128, o + 256), slice(o, o + 256))
            lead[at] = lead[at] - w * tbuf[child, 128:256, :]

    @pl.loop(0, 4)
    def _(kb):
        at = aligned(kb * 128, 128)
        left, right = pivot_block(lead[at, at], lambda: ring_p[0].step(kb))
        for i in range(16):
            ut[8 * i : 8 * i + 8, :] = left[i]
            vt[kb, 8 * i : 8 * i + 8, :] = right[i]
        ring_p[1].step(kb)
        ring_g.step(kb)

        @pl.when(kb < 3)
        def _():
            spread_p.forward(2 * kb + 1)
            spread_p.forward(2 * kb + 2)

        @pl.when(kb == 3)
        def _():
            spread_p.forward(7)

        @pl.when(kb == 1)
        def _():
            e_half.wait_recv()
            e_share.start()

            @pl.when(jnp.logical_not(leads))
            def _():
                own_entries()

            for q in range(16):
                both[32 * q : 32 * q + 32, 512:1024] = fbuf[q, 1].astype(f32)

        row_id = lax.broadcasted_iota(jnp.int32, (512, 128), 0)
        panel = hdot(lead[:, at], vt[kb], NT)
        panel = jnp.where(row_id >= (kb + 1) * 128, panel, 0.0)
        lead[...] = lead[...] - hdot(panel, panel, NT)
        lead[:, at] = panel
        lead[at, at] = ut[...].T

    spread_p.finish()
    e_share.wait_recv()
    for h in range(8):
        both[64 * h : 64 * h + 64, 0:512] = gbuf[h].astype(f32)
    for child in range(2):
        here = jnp.concatenate([prow[kz, child] for kz in range(8)], axis=1)
        there = jnp.concatenate([pcol[2 * kz + child] for kz in range(8)], axis=1)
        first = panel_0(child)
        schur = across(here, there)
        row_part = across(first, here)
        col_part = across(first, there)
        lo = map_ref[child, 0]
        ro = map_ref[child, group] - 2 * group
        co = map_ref[child, c] - 2 * c
        for i in range(2):
            w = (lo == i).astype(f32)
            for k in range(2):
                tile[quarter(i, k)] = tile[quarter(i, k)] - weight(child, i, k) * schur
                at = quarter(i, k)
                both[at] = both[at] - w * (ro == k).astype(f32) * row_part
                at = quarter(i, k + 2)
                both[at] = both[at] - w * (co == k).astype(f32) * col_part

    @pl.when(c == 0)
    def _():
        both[:, 0:512] = tile[...].T

    for kb in range(4):
        at = slice(128 * kb, 128 * kb + 128)
        done = hdot(vt[kb], both[at, :], NN)
        both[at, :] = done
        if kb < 3:
            below = slice(128 * kb + 128, 512)
            both[below, :] = both[below, :] - hdot(lead[below, at], done, NN)

    @pl.when(leads)
    def _():
        row_id = lax.broadcasted_iota(jnp.int32, (512, 512), 0)
        col_id = lax.broadcasted_iota(jnp.int32, (512, 512), 1)
        keep = jnp.logical_and(c == 0, col_id <= row_id)
        o_ref[...] = jnp.where(keep, lead[...], 0.0)

    @pl.when(jnp.logical_and(jnp.logical_not(leads), c == 0))
    def _():
        o_ref[...] = both[:, 0:512].T

    @pl.when(jnp.logical_and(jnp.logical_not(leads), c != 0))
    def _():
        o_ref[...] = tile[...] - hdot(both[:, 0:512], both[:, 512:1024], TN)

    @pl.when(r == 0)
    def _():
        for copy in fa_copies:
            copy.wait_send()

    @pl.when(root)
    def _():
        for copy in rs_copies[1:]:
            copy.wait_send()

    @pl.when(leads)
    def _():
        for copy in cs_copies[1:] + gs_copies[1:]:
            copy.wait_send()

        @pl.when(c != 0)
        def _():
            gs_copies[0].wait_send()

    @pl.when(c == 0)
    def _():
        for copy in rp_copies[1:]:
            copy.wait_send()

    for entry in u_copies + own_copies:
        @pl.when(jnp.logical_not(entry[0]))
        def _():
            entry[1].wait_send()

    for copy in fb_copies + d1_copies + [cpl_rem, inv_rem, inv_share, e_half, e_share]:
        copy.wait_send()
    for gather in (*ring_c, *ring_p, ring_g, spread_0, spread_f, spread_p):
        gather.drain()


def local(child_update, child_coupling, pivot_inverse, child_map, parent_front, block_pattern):
    vmem = pl.BlockSpec(memory_space=pltpu.VMEM)
    smem = pl.BlockSpec(memory_space=pltpu.SMEM)
    hbm = pl.BlockSpec(memory_space=pl.ANY)
    dma = pltpu.SemaphoreType.DMA

    def pair(n, m):
        return [dma((n,)), dma((m,))]

    return pl.pallas_call(
        kernel,
        out_shape=jax.ShapeDtypeStruct((512, 512), f32),
        in_specs=[smem, smem, hbm, hbm, hbm, hbm],
        out_specs=vmem,
        scratch_shapes=[
            pltpu.VMEM((2, 128, 2048), bf16),
            pltpu.VMEM((8, 2, 256, 128), bf16),
            pltpu.VMEM((256, 256), bf16),
            pltpu.VMEM((8, 2, 256, 256), bf16),
            pltpu.VMEM((16, 256, 256), bf16),
            pltpu.VMEM((2, 256, 256), f32),
            pltpu.VMEM((512, 512), f32),
            pltpu.VMEM((512, 512), f32),
            pltpu.VMEM((512, 512), bf16),
            pltpu.VMEM((16, 2, 32, 512), bf16),
            pltpu.VMEM((8, 64, 512), bf16),
            pltpu.VMEM((16, 32, 128), bf16),
            pltpu.VMEM((2, 8, 256, 256), bf16),
            pltpu.VMEM((2, 256, 256), f32),
            pltpu.VMEM((512, 512), f32),
            pltpu.VMEM((512, 1024), f32),
            pltpu.VMEM((128, 128), f32),
            pltpu.VMEM((4, 128, 128), f32),
            dma((3,)), *pair(8, 1), *pair(16, 16), *pair(16, 16), *pair(8, 8),
            *pair(2, 2), *pair(3, 3), *pair(2, 2), dma((2, 8)), dma((2, 8)), dma((2, 8)), dma((2, 8)),
            *pair(8, 8), *pair(2, 2), *pair(1, 1), *pair(16, 16), *pair(16, 16),
            *pair(16, 1), *pair(16, 1), *pair(16, 1), *pair(16, 1), *pair(2, 2),
        ],
        compiler_params=pltpu.CompilerParams(
            has_side_effects=True, collective_id=0, vmem_limit_bytes=60 * 1024 * 1024
        ),
        cost_estimate=pl.CostEstimate(
            flops=8_000_000_000, bytes_accessed=4_000_000, transcendentals=512
        ),
    )(child_map, block_pattern, child_update, child_coupling, pivot_inverse, parent_front)


def solution(mesh):
    return jax.shard_map(
        local,
        mesh=mesh,
        in_specs=(
            P("sub", "row", "col"),
            P("sub", "row", "col"),
            P("sub", "col", None),
            P(),
            P(("sub", "row"), "col"),
            P(("sub", "row"), "col"),
        ),
        out_specs=P(("sub", "row"), "col"),
        check_vma=False,
    )
```

```python
import jax
import jax.numpy as jnp
from jax import lax
from jax.experimental import pallas as pl
from jax.experimental.pallas import tpu as pltpu
from jax.sharding import PartitionSpec as P

f32 = jnp.float32
bf16 = jnp.bfloat16
MESH = pl.DeviceIdType.MESH
NT = (((1,), (1,)), ((), ()))
NN = (((1,), (0,)), ((), ()))
TN = (((0,), (0,)), ((), ()))


def rcopy(src, dst, send, recv, dev):
    return pltpu.make_async_remote_copy(
        src_ref=src, dst_ref=dst, send_sem=send, recv_sem=recv, device_id=dev, device_id_type=MESH
    )


def aligned(start, size):
    return pl.ds(pl.multiple_of(start, size), size)


class Ring:
    def __init__(self, slot, send, recv, right_last, s, r, xlo, z):
        self.slot, self.send, self.recv, self.z = slot, send, recv, z
        self.right_last = right_last
        self.to_right = (s, r, xlo * 8 + lax.rem(z + 1, 8))
        self.to_left = (s, r, xlo * 8 + lax.rem(z + 7, 8))

    def right(self, t):
        slot = self.slot(lax.rem(self.z - t + 8, 8))
        return rcopy(slot, slot, self.send.at[t], self.recv.at[t], self.to_right)

    def left(self, t):
        slot = self.slot(lax.rem(self.z + t, 8))
        return rcopy(slot, slot, self.send.at[4 + t], self.recv.at[4 + t], self.to_left)

    def both(self, t, act):
        long, short = (self.right, self.left) if self.right_last else (self.left, self.right)
        act(long(t))
        if isinstance(t, int):
            if t < 3:
                act(short(t))
        else:

            @pl.when(t < 3)
            def _():
                act(short(t))

    def start(self, t):
        self.both(t, lambda copy: copy.start())

    def arrive(self, t):
        self.both(t, lambda copy: copy.wait_recv())

    def step(self, t):
        self.arrive(t)
        if isinstance(t, int):
            if t < 3:
                self.start(t + 1)
        else:

            @pl.when(t < 3)
            def _():
                self.start(t + 1)

    def drain(self):
        for t in range(4):
            self.both(t, lambda copy: copy.wait_send())


class Spread:
    def __init__(self, slot, send, recv, s, r, c):
        self.slot, self.send, self.recv = slot, send, recv
        self.s, self.r, self.c = s, r, c
        self.y, self.core = r // 2, lax.rem(r, 2)

    def piece(self, side, back):
        side = self.s if side == 0 else 1 - self.s
        return self.slot(side, 2 * lax.rem(self.y - back + 4, 4) + self.core)

    def copy(self, ref, sem, dev):
        return rcopy(ref, ref, self.send.at[sem], self.recv.at[sem], dev)

    def hop(self):
        return self.copy(self.piece(0, 0), 0, (1 - self.s, self.r, self.c))

    def along(self, side, d):
        to = (self.s, 2 * lax.rem(self.y + d, 4) + self.core, self.c)
        return self.copy(self.piece(side, 0), 3 * side + d, to)

    def share(self, side, d):
        to = (self.s, self.r + 1 - 2 * self.core, self.c)
        return self.copy(self.piece(side, d), 7 + 4 * side + d, to)

    def start(self):
        for d in range(1, 4):
            self.along(0, d).start()
        self.share(0, 0).start()

    def relay(self):
        self.hop().wait_recv()
        for d in range(1, 4):
            self.along(1, d).start()
        self.share(1, 0).start()

    def forward(self, side):
        for d in range(1, 4):
            self.along(side, d).wait_recv()
            self.share(side, d).start()

    def finish(self, side):
        for d in range(4):
            self.share(side, d).wait_recv()

    def drain(self):
        self.hop().wait_send()
        for side in range(2):
            for d in range(4):
                if d:
                    self.along(side, d).wait_send()
                self.share(side, d).wait_send()


class Direct:
    def __init__(self, slot, send, recv, n, chip, core, device, partner):
        self.slot, self.send, self.recv, self.n = slot, send, recv, n
        self.chip, self.core, self.device, self.partner = chip, core, device, partner

    def out(self, d):
        own = self.slot(2 * self.chip + self.core)
        to = lax.rem(self.chip + d, self.n)
        return rcopy(own, own, self.send.at[d], self.recv.at[d], self.device(to))

    def share(self, d):
        slot = self.slot(2 * lax.rem(self.chip - d + self.n, self.n) + self.core)
        return rcopy(slot, slot, self.send.at[self.n + d], self.recv.at[self.n + d], self.partner)

    def start(self):
        for d in range(1, self.n):
            self.out(d).start()
        self.share(0).start()

    def forward(self, d):
        self.out(d).wait_recv()
        self.share(d).start()

    def finish(self):
        for d in range(self.n):
            self.share(d).wait_recv()

    def drain(self):
        for d in range(1, self.n):
            self.out(d).wait_send()
        for d in range(self.n):
            self.share(d).wait_send()


def lanes(x, k):
    return jnp.broadcast_to(x[:, k : k + 1], (8, 128))


def rows(x, k):
    return jnp.broadcast_to(x[k : k + 1, :], (8, 128))


def pivot_block(d, hook):
    left = [d[8 * i : 8 * i + 8, :] for i in range(16)]
    rid = lax.broadcasted_iota(jnp.int32, (8, 128), 0)
    cid = lax.broadcasted_iota(jnp.int32, (8, 128), 1)
    right = [(cid == rid + 8 * i).astype(f32) for i in range(16)]
    for b in range(16):
        lead = [lanes(left[b], 8 * b + k) for k in range(8)]
        lo, ro = left[b], right[b]
        top, inv, row_l, row_r = {}, [], [], []
        for k in range(8):
            rinv = lax.rsqrt(rows(lead[k], k))
            f = jnp.where(rid > k, lead[k] * rinv, 0.0)
            for m in range(k + 1, 8):
                top[k, m] = rows(lead[m], k) * rinv
                lead[m] = lead[m] - f * top[k, m]
            row_l.append(rows(lo, k) * rinv)
            row_r.append(rows(ro, k) * rinv)
            lo = lo - f * row_l[k]
            ro = ro - f * row_r[k]
            inv.append(rinv)
        left[b], right[b] = row_l[0], row_r[0]
        for k in range(1, 8):
            left[b] = jnp.where(rid == k, row_l[k], left[b])
            right[b] = jnp.where(rid == k, row_r[k], right[b])
        for i in range(b + 1, 16):
            own = [lanes(left[i], 8 * b + k) for k in range(8)]
            lo, ro = left[i], right[i]
            for k in range(8):
                f = own[k] * inv[k]
                for m in range(k + 1, 8):
                    own[m] = own[m] - f * top[k, m]
                lo = lo - f * row_l[k]
                ro = ro - f * row_r[k]
            left[i], right[i] = lo, ro
        if b == 5:
            hook()
    return left, right


def halves(x):
    high = x.astype(bf16)
    return high, (x - high.astype(f32)).astype(bf16)


def hdot(a, b, dims):
    (ah, al), (bh, bl) = halves(a), halves(b)

    def part(x, y):
        return lax.dot_general(x, y, dims, preferred_element_type=f32)

    return part(ah, bh) + (part(ah, bl) + part(al, bh))


def kernel(
    map_ref, pat_ref, upd_ref, cpl_ref, inv_ref, front_ref, o_ref,
    invbuf, cbuf, ptile, prow, pcol, ubuf, front, tile, fsrc, fbuf, gbuf,
    fc, p0, tbuf, lead, both, ut, vt,
    loc_sem, fa_send, fa_recv, fb_send, fb_recv, d1_send, d1_recv, d2_send, d2_recv,
    t_send, t_recv, x_send, x_recv, u_send, u_recv, c_send, c_recv, p_send, p_recv,
    g_send, g_recv, pr_send, pr_recv, pc_send, pc_recv, k1_send, k1_recv, kf_send, kf_recv,
    rs_send, rs_recv, rp_send, rp_recv, gs_send, gs_recv, cs_send, cs_recv,
):
    s, r, c = lax.axis_index("sub"), lax.axis_index("row"), lax.axis_index("col")
    xlo, z = c // 8, lax.rem(c, 8)
    y, core = r // 2, lax.rem(r, 2)
    group = 8 * s + r
    chip = 4 * s + y
    leads = group == 0
    root = jnp.logical_and(leads, c == 0)
    block = 2 * r + xlo
    xpart = (s, r, lax.rem(c + 8, 16))
    cpart = (s, r + 1 - 2 * core, c)
    hpart = (1 - s, r, c)

    def at_group(g):
        return (g // 8, lax.rem(g, 8), c)

    inv_loc = pltpu.make_async_copy(inv_ref.at[0], invbuf.at[xlo], loc_sem.at[0])
    mine, theirs = aligned(xlo * 256, 256), aligned(256 - xlo * 256, 256)
    cpl_loc = pltpu.make_async_copy(cpl_ref.at[0, mine], cbuf.at[z, xlo], loc_sem.at[1])
    front_loc = pltpu.make_async_copy(front_ref, front, loc_sem.at[2])
    inv_loc.start()
    cpl_loc.start()
    front_loc.start()

    barrier = pltpu.get_barrier_semaphore()

    def same(dev):
        return jnp.logical_and(jnp.logical_and(dev[0] == s, dev[1] == r), dev[2] == c)

    def hello(dev):
        pl.semaphore_signal(barrier, inc=1, device_id=dev, device_id_type=MESH)

    def hello_other(dev):
        @pl.when(jnp.logical_not(same(dev)))
        def _():
            hello(dev)

    for d in range(1, 16):
        hello((s, r, lax.rem(c + d, 16)))
        hello(at_group(lax.rem(group + d, 16)))
    half_block = group // 2
    for child in range(2):
        hello_other((child, half_block, lax.rem(group, 2) * 8 + z))
    hello_other((core, c // 2, lax.rem(c, 2) * 8 + chip))
    hello_other((0, 0, group))
    pr_dest = [(block // 8, lax.rem(block, 8), xh * 8 + z) for xh in range(2)]
    pc_dest = (z // 4, 2 * lax.rem(z, 4) + s, block)

    def other(dev):
        return jnp.where(same(dev), 0, 1)

    expected = 30 + other(pr_dest[0]) + other(pr_dest[1]) + other(pc_dest)
    expected = expected + jnp.where(leads, 16 - jnp.where(c == 0, 1, 0), 0)
    pl.semaphore_wait(barrier, expected)

    fa_copies = [
        rcopy(cpl_ref.at[0, pl.ds(32 * q, 32)], fc.at[c], fa_send.at[q], fa_recv.at[0], (s, q, c))
        for q in range(1, 8)
    ]
    u_copies = []
    for i in range(2):
        dest = at_group(2 * r + i)
        u_copies.append((same(dest), rcopy(
            upd_ref.at[0, pl.ds(256 * i, 256)], ubuf.at[s], u_send.at[i], u_recv.at[s], dest
        ), i))

    def u_start(entry):
        own, rem, i = entry

        @pl.when(own)
        def _():
            pltpu.make_async_copy(
                upd_ref.at[0, pl.ds(256 * i, 256)], ubuf.at[s], u_recv.at[s]
            ).start()

        @pl.when(jnp.logical_not(own))
        def _():
            rem.start()

    @pl.when(r == 0)
    def _():
        for copy in fa_copies:
            copy.start()
        pltpu.make_async_copy(cpl_ref.at[0, pl.ds(0, 32)], fc.at[c], fa_recv.at[0]).start()
        u_start(u_copies[0])

    cpl_rem = rcopy(cpl_ref.at[0, theirs], cbuf.at[z, xlo], x_send.at[1], x_recv.at[1], xpart)
    cpl_rem.start()
    inv_half = aligned(64 * core, 64)
    inv_rem = rcopy(
        inv_ref.at[0, inv_half], invbuf.at[xlo, inv_half], x_send.at[0], x_recv.at[0], xpart
    )
    inv_rem.start()

    rcopy(fc.at[c], fc.at[c], fa_send.at[0], fa_recv.at[0], xpart).wait_recv()
    fb_copies = [
        rcopy(fc.at[c], fc.at[c], fb_send.at[d], fb_recv.at[d], (s, r, lax.rem(c + d, 16)))
        for d in range(1, 16)
    ]
    for copy in fb_copies:
        copy.start()

    cpl_loc.wait()
    cpl_rem.wait_recv()
    ring_c = [
        Ring(lambda q, kh=kh: cbuf.at[q, kh], c_send.at[kh], c_recv.at[kh], kh == 0, s, r, xlo, z)
        for kh in range(2)
    ]
    for ring in ring_c:
        ring.start(0)

    @pl.when(r != 0)
    def _():
        u_start(u_copies[0])

    u_start(u_copies[1])
    for ring in ring_c:
        ring.step(0)

    def weight(child, i, k):
        ro = map_ref[child, group] - 2 * group
        co = map_ref[child, c] - 2 * c
        return (ro == i).astype(f32) * (co == k).astype(f32)

    def quarter(i, k):
        return (slice(256 * i, 256 * i + 256), slice(256 * k, 256 * k + 256))

    def own_entries():
        for child in range(2):
            slot = ubuf.at[child]
            rcopy(slot, slot, u_send.at[0], u_recv.at[child], xpart).wait_recv()
        for i in range(2):
            for k in range(2):
                value = front[quarter(i, k)] * pat_ref[i, k].astype(f32)
                for child in range(2):
                    value = value + weight(child, i, k) * ubuf[child]
                tile[quarter(i, k)] = value

    front_loc.wait()
    gs_copies, cs_copies, rs_copies = [], [], []
    for cp in range(16):
        gs_copies.append(rcopy(
            fsrc.at[pl.ds(64 * (cp % 8), 64)], gbuf.at[cp % 8],
            gs_send.at[cp], gs_recv.at[0], (c // 8, lax.rem(c, 8), cp),
        ))
        piece = fsrc.at[pl.ds(32 * cp, 32)]
        cs_copies.append(rcopy(
            piece, fbuf.at[cp, 1], cs_send.at[cp], cs_recv.at[0], (cp // 8, cp % 8, c)
        ))
        rs_copies.append(rcopy(
            piece, fbuf.at[cp, 0], rs_send.at[cp], rs_recv.at[0], (cp // 8, cp % 8, 0)
        ))

    for copy in fb_copies:
        copy.wait_recv()
    inv_loc.wait()
    wide = jnp.concatenate([fc[i] for i in range(16)], axis=1)
    piece = lax.dot_general(wide, invbuf[xlo], NT, preferred_element_type=f32).astype(bf16)
    my_rows = aligned(32 * r, 32)
    p0[s, z, my_rows, aligned(128 * xlo, 128)] = piece
    d1_copies = []
    for d in range(1, 16):
        slot = p0.at[s, z, my_rows, aligned(128 * xlo, 128)]
        d1_copies.append(rcopy(
            slot, slot, d1_send.at[d], d1_recv.at[d], (s, r, lax.rem(c + d, 16))
        ))
    for copy in d1_copies:
        copy.start()

    for ring in ring_c:
        ring.step(1)
    inv_rem.wait_recv()
    other_half = invbuf.at[1 - xlo, inv_half]
    inv_share = rcopy(other_half, other_half, x_send.at[2], x_recv.at[2], cpart)
    inv_share.start()

    @pl.when(leads)
    def _():
        own_entries()
        fsrc[...] = tile[...].astype(bf16)

        @pl.when(c == 0)
        def _():
            for copy in rs_copies[1:]:
                copy.start()
            pltpu.make_async_copy(fsrc.at[pl.ds(0, 32)], fbuf.at[0, 0], rs_recv.at[0]).start()
            pltpu.make_async_copy(fsrc.at[pl.ds(0, 64)], gbuf.at[0], gs_recv.at[0]).start()

        pltpu.make_async_copy(fsrc.at[pl.ds(0, 32)], fbuf.at[0, 1], cs_recv.at[0]).start()
        for copy in cs_copies[1:]:
            copy.start()

        @pl.when(c != 0)
        def _():
            gs_copies[0].start()

        for copy in gs_copies[1:]:
            copy.start()

    for ring in ring_c:
        ring.step(2)
    for copy in d1_copies:
        copy.wait_recv()
    spread_0 = Spread(
        lambda side, q: p0.at[side, :, aligned(32 * q, 32), :], d2_send, d2_recv, s, r, c
    )
    spread_0.start()

    rp_copies = [
        rcopy(fbuf.at[group, 0], fbuf.at[group, 0], rp_send.at[d], rp_recv.at[0], (s, r, d))
        for d in range(16)
    ]

    @pl.when(c == 0)
    def _():
        slot = fbuf.at[group, 0]
        rcopy(slot, slot, rs_send.at[0], rs_recv.at[0], xpart).wait_recv()
        for copy in rp_copies[1:]:
            copy.start()

    inv_share.wait_recv()
    for ring in ring_c:
        ring.step(3)
    wide = jnp.concatenate([cbuf[q % 8, q // 8] for q in range(16)], axis=1)
    for half in range(2):
        total = lax.dot_general(wide, invbuf[half], NT, preferred_element_type=f32)
        ptile[:, 128 * half : 128 * half + 128] = total.astype(bf16)

    own_copies = []
    for xh in range(2):
        slot = prow.at[z, s]
        own_copies.append((
            same(pr_dest[xh]), rcopy(ptile, slot, pr_send.at[xh], pr_recv.at[s], pr_dest[xh]),
            slot, pr_recv.at[s],
        ))
    slot = pcol.at[2 * z + s]
    own_copies.append((
        same(pc_dest), rcopy(ptile, slot, pc_send.at[0], pc_recv.at[0], pc_dest),
        slot, pc_recv.at[0],
    ))
    for own, rem, slot, sem in own_copies:
        @pl.when(own)
        def _():
            pltpu.make_async_copy(ptile, slot, sem).start()

        @pl.when(jnp.logical_not(own))
        def _():
            rem.start()

    spread_0.forward(0)
    spread_0.finish(0)

    def across(left, right):
        return lax.dot_general(left, right, NT, preferred_element_type=f32)

    def panel_0(child):
        return jnp.concatenate([p0[child, kz] for kz in range(8)], axis=1)

    wide = panel_0(s)
    tbuf[s] = across(wide, wide)
    t_parts = [tbuf.at[s, pl.ds(128, 128)], tbuf.at[s, pl.ds(0, 128), pl.ds(0, 128)]]
    t_copies = [rcopy(t_parts[i], t_parts[i], t_send.at[i], t_recv.at[i], hpart) for i in range(2)]
    for copy in t_copies:
        copy.start()

    slot = fbuf.at[group, 1]
    rcopy(slot, slot, cs_send.at[0], cs_recv.at[0], xpart).wait_recv()

    @pl.when(c != 0)
    def _():
        rp_copies[0].wait_recv()

    spread_f = Direct(
        lambda q: fbuf.at[q], kf_send, kf_recv, 8, chip, core,
        lambda to: at_group(2 * to + core), cpart,
    )
    spread_f.start()

    for child in range(2):
        slot = prow.at[z, child]
        rcopy(slot, slot, pr_send.at[0], pr_recv.at[child], xpart).wait_recv()
    ring_p = [
        Ring(
            lambda q, child=child: prow.at[q, child],
            p_send.at[child], p_recv.at[child], child == 0, s, r, xlo, z,
        )
        for child in range(2)
    ]
    for ring in ring_p:
        ring.start(0)
    rcopy(pcol.at[group], pcol.at[group], pc_send.at[0], pc_recv.at[0], xpart).wait_recv()
    spread_p = Spread(lambda side, q: pcol.at[8 * side + q], k1_send, k1_recv, s, r, c)
    spread_p.hop().start()
    spread_p.start()
    spread_0.hop().start()
    ring_g = Ring(lambda q: gbuf.at[q], g_send, g_recv, True, s, r, xlo, z)
    rcopy(gbuf.at[z], gbuf.at[z], gs_send.at[0], gs_recv.at[0], xpart).wait_recv()
    ring_g.start(0)
    for d in range(1, 8):
        spread_f.forward(d)
    spread_f.finish()
    for copy in t_copies:
        copy.wait()
    spread_p.relay()

    @pl.when(root)
    def _():
        lead[...] = tile[...]

    @pl.when(jnp.logical_not(root))
    def _():
        for q in range(16):
            lead[32 * q : 32 * q + 32, :] = fbuf[q, 0].astype(f32)

    for child in range(2):
        for i in range(2):
            w = (map_ref[child, 0] == i).astype(f32)
            o = 256 * i
            at = (slice(o, o + 128), slice(o, o + 128))
            lead[at] = lead[at] - w * tbuf[child, 0:128, 0:128]
            at = (slice(o + 128, o + 256), slice(o, o + 256))
            lead[at] = lead[at] - w * tbuf[child, 128:256, :]

    @pl.loop(0, 4)
    def _(kb):
        at = aligned(kb * 128, 128)
        left, right = pivot_block(lead[at, at], lambda: ring_p[0].step(kb))
        for i in range(16):
            ut[8 * i : 8 * i + 8, :] = left[i]
            vt[kb, 8 * i : 8 * i + 8, :] = right[i]
        ring_p[1].step(kb)
        ring_g.step(kb)

        @pl.when(kb == 0)
        def _():
            spread_p.forward(0)
            spread_0.relay()

        @pl.when(kb == 1)
        def _():
            spread_p.forward(1)
            spread_0.forward(1)

            @pl.when(jnp.logical_not(leads))
            def _():
                own_entries()

            for q in range(16):
                both[32 * q : 32 * q + 32, 512:1024] = fbuf[q, 1].astype(f32)

        row_id = lax.broadcasted_iota(jnp.int32, (512, 128), 0)
        panel = hdot(lead[:, at], vt[kb], NT)
        panel = jnp.where(row_id >= (kb + 1) * 128, panel, 0.0)
        lead[...] = lead[...] - hdot(panel, panel, NT)
        lead[:, at] = panel
        lead[at, at] = ut[...].T

    for side in range(2):
        spread_p.finish(side)
    spread_0.finish(1)
    for h in range(8):
        both[64 * h : 64 * h + 64, 0:512] = gbuf[h].astype(f32)
    for child in range(2):
        here = jnp.concatenate([prow[kz, child] for kz in range(8)], axis=1)
        there = jnp.concatenate([pcol[2 * kz + child] for kz in range(8)], axis=1)
        first = panel_0(child)
        schur = across(here, there)
        row_part = across(first, here)
        col_part = across(first, there)
        lo = map_ref[child, 0]
        ro = map_ref[child, group] - 2 * group
        co = map_ref[child, c] - 2 * c
        for i in range(2):
            w = (lo == i).astype(f32)
            for k in range(2):
                tile[quarter(i, k)] = tile[quarter(i, k)] - weight(child, i, k) * schur
                at = quarter(i, k)
                both[at] = both[at] - w * (ro == k).astype(f32) * row_part
                at = quarter(i, k + 2)
                both[at] = both[at] - w * (co == k).astype(f32) * col_part

    @pl.when(c == 0)
    def _():
        both[:, 0:512] = tile[...].T

    for kb in range(4):
        at = slice(128 * kb, 128 * kb + 128)
        done = hdot(vt[kb], both[at, :], NN)
        both[at, :] = done
        if kb < 3:
            below = slice(128 * kb + 128, 512)
            both[below, :] = both[below, :] - hdot(lead[below, at], done, NN)

    @pl.when(leads)
    def _():
        row_id = lax.broadcasted_iota(jnp.int32, (512, 512), 0)
        col_id = lax.broadcasted_iota(jnp.int32, (512, 512), 1)
        keep = jnp.logical_and(c == 0, col_id <= row_id)
        o_ref[...] = jnp.where(keep, lead[...], 0.0)

    @pl.when(jnp.logical_and(jnp.logical_not(leads), c == 0))
    def _():
        o_ref[...] = both[:, 0:512].T

    @pl.when(jnp.logical_and(jnp.logical_not(leads), c != 0))
    def _():
        o_ref[...] = tile[...] - hdot(both[:, 0:512], both[:, 512:1024], TN)

    @pl.when(r == 0)
    def _():
        for copy in fa_copies:
            copy.wait_send()

    @pl.when(root)
    def _():
        for copy in rs_copies[1:]:
            copy.wait_send()

    @pl.when(leads)
    def _():
        for copy in cs_copies[1:] + gs_copies[1:]:
            copy.wait_send()

        @pl.when(c != 0)
        def _():
            gs_copies[0].wait_send()

    @pl.when(c == 0)
    def _():
        for copy in rp_copies[1:]:
            copy.wait_send()

    for entry in u_copies + own_copies:
        @pl.when(jnp.logical_not(entry[0]))
        def _():
            entry[1].wait_send()

    for copy in fb_copies + d1_copies + [cpl_rem, inv_rem, inv_share]:
        copy.wait_send()
    for gather in (*ring_c, *ring_p, ring_g, spread_0, spread_f, spread_p):
        gather.drain()


def local(child_update, child_coupling, pivot_inverse, child_map, parent_front, block_pattern):
    vmem = pl.BlockSpec(memory_space=pltpu.VMEM)
    smem = pl.BlockSpec(memory_space=pltpu.SMEM)
    hbm = pl.BlockSpec(memory_space=pl.ANY)
    dma = pltpu.SemaphoreType.DMA

    def pair(n, m):
        return [dma((n,)), dma((m,))]

    return pl.pallas_call(
        kernel,
        out_shape=jax.ShapeDtypeStruct((512, 512), f32),
        in_specs=[smem, smem, hbm, hbm, hbm, hbm],
        out_specs=vmem,
        scratch_shapes=[
            pltpu.VMEM((2, 128, 2048), bf16),
            pltpu.VMEM((8, 2, 256, 128), bf16),
            pltpu.VMEM((256, 256), bf16),
            pltpu.VMEM((8, 2, 256, 256), bf16),
            pltpu.VMEM((16, 256, 256), bf16),
            pltpu.VMEM((2, 256, 256), f32),
            pltpu.VMEM((512, 512), f32),
            pltpu.VMEM((512, 512), f32),
            pltpu.VMEM((512, 512), bf16),
            pltpu.VMEM((16, 2, 32, 512), bf16),
            pltpu.VMEM((8, 64, 512), bf16),
            pltpu.VMEM((16, 32, 128), bf16),
            pltpu.VMEM((2, 8, 256, 256), bf16),
            pltpu.VMEM((2, 256, 256), f32),
            pltpu.VMEM((512, 512), f32),
            pltpu.VMEM((512, 1024), f32),
            pltpu.VMEM((128, 128), f32),
            pltpu.VMEM((4, 128, 128), f32),
            dma((3,)), *pair(8, 1), *pair(16, 16), *pair(16, 16), *pair(15, 15),
            *pair(2, 2), *pair(3, 3), *pair(2, 2), dma((2, 8)), dma((2, 8)), dma((2, 8)), dma((2, 8)),
            *pair(8, 8), *pair(2, 2), *pair(1, 1), *pair(16, 16), *pair(16, 16),
            *pair(16, 1), *pair(16, 1), *pair(16, 1), *pair(16, 1),
        ],
        compiler_params=pltpu.CompilerParams(
            has_side_effects=True, collective_id=0, vmem_limit_bytes=60 * 1024 * 1024
        ),
        cost_estimate=pl.CostEstimate(
            flops=8_000_000_000, bytes_accessed=4_000_000, transcendentals=512
        ),
    )(child_map, block_pattern, child_update, child_coupling, pivot_inverse, parent_front)


def solution(mesh):
    return jax.shard_map(
        local,
        mesh=mesh,
        in_specs=(
            P("sub", "row", "col"),
            P("sub", "row", "col"),
            P("sub", "col", None),
            P(),
            P(("sub", "row"), "col"),
            P(("sub", "row"), "col"),
        ),
        out_specs=P(("sub", "row"), "col"),
        check_vma=False,
    )
```

```python
import jax
import jax.numpy as jnp
from jax import lax
from jax.experimental import pallas as pl
from jax.experimental.pallas import tpu as pltpu
from jax.sharding import PartitionSpec as P

f32 = jnp.float32
bf16 = jnp.bfloat16
MESH = pl.DeviceIdType.MESH
NT = (((1,), (1,)), ((), ()))
NN = (((1,), (0,)), ((), ()))
TN = (((0,), (0,)), ((), ()))


def rcopy(src, dst, send, recv, dev):
    return pltpu.make_async_remote_copy(
        src_ref=src, dst_ref=dst, send_sem=send, recv_sem=recv, device_id=dev, device_id_type=MESH
    )


def aligned(start, size):
    return pl.ds(pl.multiple_of(start, size), size)


class Ring:
    def __init__(self, slot, send, recv, right_last, s, r, xlo, z):
        self.slot, self.send, self.recv, self.z = slot, send, recv, z
        self.right_last = right_last
        self.to_right = (s, r, xlo * 8 + lax.rem(z + 1, 8))
        self.to_left = (s, r, xlo * 8 + lax.rem(z + 7, 8))

    def right(self, t):
        slot = self.slot(lax.rem(self.z - t + 8, 8))
        return rcopy(slot, slot, self.send.at[t], self.recv.at[t], self.to_right)

    def left(self, t):
        slot = self.slot(lax.rem(self.z + t, 8))
        return rcopy(slot, slot, self.send.at[4 + t], self.recv.at[4 + t], self.to_left)

    def both(self, t, act):
        long, short = (self.right, self.left) if self.right_last else (self.left, self.right)
        act(long(t))
        if isinstance(t, int):
            if t < 3:
                act(short(t))
        else:

            @pl.when(t < 3)
            def _():
                act(short(t))

    def start(self, t):
        self.both(t, lambda copy: copy.start())

    def arrive(self, t):
        self.both(t, lambda copy: copy.wait_recv())

    def step(self, t):
        self.arrive(t)
        if isinstance(t, int):
            if t < 3:
                self.start(t + 1)
        else:

            @pl.when(t < 3)
            def _():
                self.start(t + 1)

    def drain(self):
        for t in range(4):
            self.both(t, lambda copy: copy.wait_send())


class Spread:
    def __init__(self, slot, send, recv, s, r, c):
        self.slot, self.send, self.recv = slot, send, recv
        self.s, self.r, self.c = s, r, c
        self.y, self.core = r // 2, lax.rem(r, 2)

    def piece(self, side, back):
        side = self.s if side == 0 else 1 - self.s
        return self.slot(side, 2 * lax.rem(self.y - back + 4, 4) + self.core)

    def copy(self, ref, sem, dev):
        return rcopy(ref, ref, self.send.at[sem], self.recv.at[sem], dev)

    def hop(self):
        return self.copy(self.piece(0, 0), 0, (1 - self.s, self.r, self.c))

    def along(self, side, d):
        to = (self.s, 2 * lax.rem(self.y + d, 4) + self.core, self.c)
        return self.copy(self.piece(side, 0), 3 * side + d, to)

    def share(self, side, d):
        to = (self.s, self.r + 1 - 2 * self.core, self.c)
        return self.copy(self.piece(side, d), 7 + 4 * side + d, to)

    def start(self):
        for d in range(1, 4):
            self.along(0, d).start()
        self.share(0, 0).start()

    def relay(self):
        self.hop().wait_recv()
        for d in range(1, 4):
            self.along(1, d).start()
        self.share(1, 0).start()

    def forward(self, side):
        for d in range(1, 4):
            self.along(side, d).wait_recv()
            self.share(side, d).start()

    def finish(self, side):
        for d in range(4):
            self.share(side, d).wait_recv()

    def drain(self):
        self.hop().wait_send()
        for side in range(2):
            for d in range(4):
                if d:
                    self.along(side, d).wait_send()
                self.share(side, d).wait_send()


class Direct:
    def __init__(self, slot, send, recv, n, chip, core, device, partner):
        self.slot, self.send, self.recv, self.n = slot, send, recv, n
        self.chip, self.core, self.device, self.partner = chip, core, device, partner

    def out(self, d):
        own = self.slot(2 * self.chip + self.core)
        to = lax.rem(self.chip + d, self.n)
        return rcopy(own, own, self.send.at[d], self.recv.at[d], self.device(to))

    def share(self, d):
        slot = self.slot(2 * lax.rem(self.chip - d + self.n, self.n) + self.core)
        return rcopy(slot, slot, self.send.at[self.n + d], self.recv.at[self.n + d], self.partner)

    def start(self):
        for d in range(1, self.n):
            self.out(d).start()
        self.share(0).start()

    def forward(self, d):
        self.out(d).wait_recv()
        self.share(d).start()

    def finish(self):
        for d in range(self.n):
            self.share(d).wait_recv()

    def drain(self):
        for d in range(1, self.n):
            self.out(d).wait_send()
        for d in range(self.n):
            self.share(d).wait_send()


def lanes(x, k):
    return jnp.broadcast_to(x[:, k : k + 1], (8, 128))


def rows(x, k):
    return jnp.broadcast_to(x[k : k + 1, :], (8, 128))


def pivot_block(d, hook):
    left = [d[8 * i : 8 * i + 8, :] for i in range(16)]
    rid = lax.broadcasted_iota(jnp.int32, (8, 128), 0)
    cid = lax.broadcasted_iota(jnp.int32, (8, 128), 1)
    right = [(cid == rid + 8 * i).astype(f32) for i in range(16)]
    for b in range(16):
        lead = [lanes(left[b], 8 * b + k) for k in range(8)]
        lo, ro = left[b], right[b]
        top, inv, row_l, row_r = {}, [], [], []
        for k in range(8):
            rinv = lax.rsqrt(rows(lead[k], k))
            f = jnp.where(rid > k, lead[k] * rinv, 0.0)
            for m in range(k + 1, 8):
                top[k, m] = rows(lead[m], k) * rinv
                lead[m] = lead[m] - f * top[k, m]
            row_l.append(rows(lo, k) * rinv)
            row_r.append(rows(ro, k) * rinv)
            lo = lo - f * row_l[k]
            ro = ro - f * row_r[k]
            inv.append(rinv)
        left[b], right[b] = row_l[0], row_r[0]
        for k in range(1, 8):
            left[b] = jnp.where(rid == k, row_l[k], left[b])
            right[b] = jnp.where(rid == k, row_r[k], right[b])
        for i in range(b + 1, 16):
            own = [lanes(left[i], 8 * b + k) for k in range(8)]
            lo, ro = left[i], right[i]
            for k in range(8):
                f = own[k] * inv[k]
                for m in range(k + 1, 8):
                    own[m] = own[m] - f * top[k, m]
                lo = lo - f * row_l[k]
                ro = ro - f * row_r[k]
            left[i], right[i] = lo, ro
        if b == 5:
            hook()
    return left, right


def halves(x):
    high = x.astype(bf16)
    return high, (x - high.astype(f32)).astype(bf16)


def hdot(a, b, dims):
    (ah, al), (bh, bl) = halves(a), halves(b)

    def part(x, y):
        return lax.dot_general(x, y, dims, preferred_element_type=f32)

    return part(ah, bh) + (part(ah, bl) + part(al, bh))


def kernel(
    map_ref, pat_ref, upd_ref, cpl_ref, inv_ref, front_ref, o_ref,
    invbuf, cbuf, ptile, prow, pcol, ubuf, front, tile, fsrc, fbuf, gbuf,
    fc, p0, tbuf, lead, both, ut, vt,
    loc_sem, fa_send, fa_recv, fb_send, fb_recv, d1_send, d1_recv, d2_send, d2_recv,
    t_send, t_recv, x_send, x_recv, u_send, u_recv, c_send, c_recv, p_send, p_recv,
    g_send, g_recv, pr_send, pr_recv, pc_send, pc_recv, k1_send, k1_recv, kf_send, kf_recv,
    rs_send, rs_recv, rp_send, rp_recv, gs_send, gs_recv, cs_send, cs_recv,
):
    s, r, c = lax.axis_index("sub"), lax.axis_index("row"), lax.axis_index("col")
    xlo, z = c // 8, lax.rem(c, 8)
    y, core = r // 2, lax.rem(r, 2)
    group = 8 * s + r
    chip = 4 * s + y
    leads = group == 0
    root = jnp.logical_and(leads, c == 0)
    block = 2 * r + xlo
    xpart = (s, r, lax.rem(c + 8, 16))
    cpart = (s, r + 1 - 2 * core, c)
    hpart = (1 - s, r, c)

    def at_group(g):
        return (g // 8, lax.rem(g, 8), c)

    inv_loc = pltpu.make_async_copy(inv_ref.at[0], invbuf.at[xlo], loc_sem.at[0])
    mine, theirs = aligned(xlo * 256, 256), aligned(256 - xlo * 256, 256)
    cpl_loc = pltpu.make_async_copy(cpl_ref.at[0, mine], cbuf.at[z, xlo], loc_sem.at[1])
    front_loc = pltpu.make_async_copy(front_ref, front, loc_sem.at[2])
    inv_loc.start()
    cpl_loc.start()
    front_loc.start()

    barrier = pltpu.get_barrier_semaphore()

    def same(dev):
        return jnp.logical_and(jnp.logical_and(dev[0] == s, dev[1] == r), dev[2] == c)

    def hello(dev):
        pl.semaphore_signal(barrier, inc=1, device_id=dev, device_id_type=MESH)

    def hello_other(dev):
        @pl.when(jnp.logical_not(same(dev)))
        def _():
            hello(dev)

    for d in range(1, 16):
        hello((s, r, lax.rem(c + d, 16)))
        hello(at_group(lax.rem(group + d, 16)))
    half_block = group // 2
    for child in range(2):
        hello_other((child, half_block, lax.rem(group, 2) * 8 + z))
    hello_other((core, c // 2, lax.rem(c, 2) * 8 + chip))
    hello_other((0, 0, group))
    pr_dest = [(block // 8, lax.rem(block, 8), xh * 8 + z) for xh in range(2)]
    pc_dest = (z // 4, 2 * lax.rem(z, 4) + s, block)

    def other(dev):
        return jnp.where(same(dev), 0, 1)

    expected = 30 + other(pr_dest[0]) + other(pr_dest[1]) + other(pc_dest)
    expected = expected + jnp.where(leads, 16 - jnp.where(c == 0, 1, 0), 0)
    pl.semaphore_wait(barrier, expected)

    fa_copies = [
        rcopy(cpl_ref.at[0, pl.ds(32 * q, 32)], fc.at[c], fa_send.at[q], fa_recv.at[0], (s, q, c))
        for q in range(1, 8)
    ]
    u_copies = []
    for i in range(2):
        dest = at_group(2 * r + i)
        u_copies.append((same(dest), rcopy(
            upd_ref.at[0, pl.ds(256 * i, 256)], ubuf.at[s], u_send.at[i], u_recv.at[s], dest
        ), i))

    def u_start(entry):
        own, rem, i = entry

        @pl.when(own)
        def _():
            pltpu.make_async_copy(
                upd_ref.at[0, pl.ds(256 * i, 256)], ubuf.at[s], u_recv.at[s]
            ).start()

        @pl.when(jnp.logical_not(own))
        def _():
            rem.start()

    @pl.when(r == 0)
    def _():
        for copy in fa_copies:
            copy.start()
        pltpu.make_async_copy(cpl_ref.at[0, pl.ds(0, 32)], fc.at[c], fa_recv.at[0]).start()
        u_start(u_copies[0])

    cpl_rem = rcopy(cpl_ref.at[0, theirs], cbuf.at[z, xlo], x_send.at[1], x_recv.at[1], xpart)
    cpl_rem.start()
    inv_half = aligned(64 * core, 64)
    inv_rem = rcopy(
        inv_ref.at[0, inv_half], invbuf.at[xlo, inv_half], x_send.at[0], x_recv.at[0], xpart
    )
    inv_rem.start()

    rcopy(fc.at[c], fc.at[c], fa_send.at[0], fa_recv.at[0], xpart).wait_recv()
    fb_copies = [
        rcopy(fc.at[c], fc.at[c], fb_send.at[d], fb_recv.at[d], (s, r, lax.rem(c + d, 16)))
        for d in range(1, 16)
    ]
    for copy in fb_copies:
        copy.start()

    cpl_loc.wait()
    cpl_rem.wait_recv()
    ring_c = [
        Ring(lambda q, kh=kh: cbuf.at[q, kh], c_send.at[kh], c_recv.at[kh], kh == 0, s, r, xlo, z)
        for kh in range(2)
    ]
    for ring in ring_c:
        ring.start(0)

    @pl.when(r != 0)
    def _():
        u_start(u_copies[0])

    u_start(u_copies[1])
    for ring in ring_c:
        ring.step(0)

    def weight(child, i, k):
        ro = map_ref[child, group] - 2 * group
        co = map_ref[child, c] - 2 * c
        return (ro == i).astype(f32) * (co == k).astype(f32)

    def quarter(i, k):
        return (slice(256 * i, 256 * i + 256), slice(256 * k, 256 * k + 256))

    def own_entries():
        for child in range(2):
            slot = ubuf.at[child]
            rcopy(slot, slot, u_send.at[0], u_recv.at[child], xpart).wait_recv()
        for i in range(2):
            for k in range(2):
                value = front[quarter(i, k)] * pat_ref[i, k].astype(f32)
                for child in range(2):
                    value = value + weight(child, i, k) * ubuf[child]
                tile[quarter(i, k)] = value

    front_loc.wait()
    gs_copies, cs_copies, rs_copies = [], [], []
    for cp in range(16):
        gs_copies.append(rcopy(
            fsrc.at[pl.ds(64 * (cp % 8), 64)], gbuf.at[cp % 8],
            gs_send.at[cp], gs_recv.at[0], (c // 8, lax.rem(c, 8), cp),
        ))
        piece = fsrc.at[pl.ds(32 * cp, 32)]
        cs_copies.append(rcopy(
            piece, fbuf.at[cp, 1], cs_send.at[cp], cs_recv.at[0], (cp // 8, cp % 8, c)
        ))
        rs_copies.append(rcopy(
            piece, fbuf.at[cp, 0], rs_send.at[cp], rs_recv.at[0], (cp // 8, cp % 8, 0)
        ))

    for copy in fb_copies:
        copy.wait_recv()
    inv_loc.wait()
    wide = jnp.concatenate([fc[i] for i in range(16)], axis=1)
    piece = lax.dot_general(wide, invbuf[xlo], NT, preferred_element_type=f32).astype(bf16)
    my_rows = aligned(32 * r, 32)
    p0[s, z, my_rows, aligned(128 * xlo, 128)] = piece
    d1_copies = []
    for d in range(1, 16):
        slot = p0.at[s, z, my_rows, aligned(128 * xlo, 128)]
        d1_copies.append(rcopy(
            slot, slot, d1_send.at[d], d1_recv.at[d], (s, r, lax.rem(c + d, 16))
        ))
    for copy in d1_copies:
        copy.start()

    for ring in ring_c:
        ring.step(1)
    inv_rem.wait_recv()
    other_half = invbuf.at[1 - xlo, inv_half]
    inv_share = rcopy(other_half, other_half, x_send.at[2], x_recv.at[2], cpart)
    inv_share.start()

    @pl.when(leads)
    def _():
        own_entries()
        fsrc[...] = tile[...].astype(bf16)

        @pl.when(c == 0)
        def _():
            for copy in rs_copies[1:]:
                copy.start()
            pltpu.make_async_copy(fsrc.at[pl.ds(0, 32)], fbuf.at[0, 0], rs_recv.at[0]).start()
            pltpu.make_async_copy(fsrc.at[pl.ds(0, 64)], gbuf.at[0], gs_recv.at[0]).start()

        pltpu.make_async_copy(fsrc.at[pl.ds(0, 32)], fbuf.at[0, 1], cs_recv.at[0]).start()
        for copy in cs_copies[1:]:
            copy.start()

        @pl.when(c != 0)
        def _():
            gs_copies[0].start()

        for copy in gs_copies[1:]:
            copy.start()

    for ring in ring_c:
        ring.step(2)
    for copy in d1_copies:
        copy.wait_recv()
    spread_0 = Spread(
        lambda side, q: p0.at[side, :, aligned(32 * q, 32), :], d2_send, d2_recv, s, r, c
    )
    spread_0.start()

    rp_copies = [
        rcopy(fbuf.at[group, 0], fbuf.at[group, 0], rp_send.at[d], rp_recv.at[0], (s, r, d))
        for d in range(16)
    ]

    @pl.when(c == 0)
    def _():
        slot = fbuf.at[group, 0]
        rcopy(slot, slot, rs_send.at[0], rs_recv.at[0], xpart).wait_recv()
        for copy in rp_copies[1:]:
            copy.start()

    inv_share.wait_recv()
    for ring in ring_c:
        ring.step(3)
    wide = jnp.concatenate([cbuf[q % 8, q // 8] for q in range(16)], axis=1)
    for half in range(2):
        total = lax.dot_general(wide, invbuf[half], NT, preferred_element_type=f32)
        ptile[:, 128 * half : 128 * half + 128] = total.astype(bf16)

    own_copies = []
    for xh in range(2):
        slot = prow.at[z, s]
        own_copies.append((
            same(pr_dest[xh]), rcopy(ptile, slot, pr_send.at[xh], pr_recv.at[s], pr_dest[xh]),
            slot, pr_recv.at[s],
        ))
    slot = pcol.at[2 * z + s]
    own_copies.append((
        same(pc_dest), rcopy(ptile, slot, pc_send.at[0], pc_recv.at[0], pc_dest),
        slot, pc_recv.at[0],
    ))
    for own, rem, slot, sem in own_copies:
        @pl.when(own)
        def _():
            pltpu.make_async_copy(ptile, slot, sem).start()

        @pl.when(jnp.logical_not(own))
        def _():
            rem.start()

    spread_0.forward(0)
    ring_g = Ring(lambda q: gbuf.at[q], g_send, g_recv, True, s, r, xlo, z)
    rcopy(gbuf.at[z], gbuf.at[z], gs_send.at[0], gs_recv.at[0], xpart).wait_recv()
    ring_g.start(0)
    spread_0.finish(0)

    def across(left, right):
        return lax.dot_general(left, right, NT, preferred_element_type=f32)

    def panel_0(child):
        return jnp.concatenate([p0[child, kz] for kz in range(8)], axis=1)

    wide = panel_0(s)
    tbuf[s] = across(wide, wide)
    t_parts = [tbuf.at[s, pl.ds(128, 128)], tbuf.at[s, pl.ds(0, 128), pl.ds(0, 128)]]
    t_copies = [rcopy(t_parts[i], t_parts[i], t_send.at[i], t_recv.at[i], hpart) for i in range(2)]
    for copy in t_copies:
        copy.start()

    slot = fbuf.at[group, 1]
    rcopy(slot, slot, cs_send.at[0], cs_recv.at[0], xpart).wait_recv()

    @pl.when(c != 0)
    def _():
        rp_copies[0].wait_recv()

    spread_f = Direct(
        lambda q: fbuf.at[q], kf_send, kf_recv, 8, chip, core,
        lambda to: at_group(2 * to + core), cpart,
    )
    spread_f.start()

    for child in range(2):
        slot = prow.at[z, child]
        rcopy(slot, slot, pr_send.at[0], pr_recv.at[child], xpart).wait_recv()
    ring_p = [
        Ring(
            lambda q, child=child: prow.at[q, child],
            p_send.at[child], p_recv.at[child], child == 0, s, r, xlo, z,
        )
        for child in range(2)
    ]
    for ring in ring_p:
        ring.start(0)
    rcopy(pcol.at[group], pcol.at[group], pc_send.at[0], pc_recv.at[0], xpart).wait_recv()
    spread_p = Spread(lambda side, q: pcol.at[8 * side + q], k1_send, k1_recv, s, r, c)
    spread_p.hop().start()
    spread_p.start()
    spread_0.hop().start()
    ring_g.step(0)
    for d in range(1, 8):
        spread_f.forward(d)
    spread_f.finish()
    for copy in t_copies:
        copy.wait()
    spread_p.relay()
    ring_g.step(1)

    @pl.when(root)
    def _():
        lead[...] = tile[...]

    @pl.when(jnp.logical_not(root))
    def _():
        for q in range(16):
            lead[32 * q : 32 * q + 32, :] = fbuf[q, 0].astype(f32)

    for child in range(2):
        for i in range(2):
            w = (map_ref[child, 0] == i).astype(f32)
            o = 256 * i
            at = (slice(o, o + 128), slice(o, o + 128))
            lead[at] = lead[at] - w * tbuf[child, 0:128, 0:128]
            at = (slice(o + 128, o + 256), slice(o, o + 256))
            lead[at] = lead[at] - w * tbuf[child, 128:256, :]

    @pl.loop(0, 4)
    def _(kb):
        at = aligned(kb * 128, 128)
        left, right = pivot_block(lead[at, at], lambda: ring_p[0].step(kb))
        for i in range(16):
            ut[8 * i : 8 * i + 8, :] = left[i]
            vt[kb, 8 * i : 8 * i + 8, :] = right[i]
        ring_p[1].step(kb)

        @pl.when(kb < 2)
        def _():
            ring_g.step(kb + 2)


        @pl.when(kb == 1)
        def _():
            spread_p.forward(0)
            spread_0.relay()

        @pl.when(kb == 2)
        def _():
            spread_p.forward(1)

        @pl.when(kb == 3)
        def _():
            spread_0.forward(1)

            @pl.when(jnp.logical_not(leads))
            def _():
                own_entries()

            for q in range(16):
                both[32 * q : 32 * q + 32, 512:1024] = fbuf[q, 1].astype(f32)

        row_id = lax.broadcasted_iota(jnp.int32, (512, 128), 0)
        panel = hdot(lead[:, at], vt[kb], NT)
        panel = jnp.where(row_id >= (kb + 1) * 128, panel, 0.0)
        lead[...] = lead[...] - hdot(panel, panel, NT)
        lead[:, at] = panel
        lead[at, at] = ut[...].T

    for side in range(2):
        spread_p.finish(side)
    spread_0.finish(1)
    for h in range(8):
        both[64 * h : 64 * h + 64, 0:512] = gbuf[h].astype(f32)
    for child in range(2):
        here = jnp.concatenate([prow[kz, child] for kz in range(8)], axis=1)
        there = jnp.concatenate([pcol[2 * kz + child] for kz in range(8)], axis=1)
        first = panel_0(child)
        schur = across(here, there)
        row_part = across(first, here)
        col_part = across(first, there)
        lo = map_ref[child, 0]
        ro = map_ref[child, group] - 2 * group
        co = map_ref[child, c] - 2 * c
        for i in range(2):
            w = (lo == i).astype(f32)
            for k in range(2):
                tile[quarter(i, k)] = tile[quarter(i, k)] - weight(child, i, k) * schur
                at = quarter(i, k)
                both[at] = both[at] - w * (ro == k).astype(f32) * row_part
                at = quarter(i, k + 2)
                both[at] = both[at] - w * (co == k).astype(f32) * col_part

    @pl.when(c == 0)
    def _():
        both[:, 0:512] = tile[...].T

    for kb in range(4):
        at = slice(128 * kb, 128 * kb + 128)
        done = hdot(vt[kb], both[at, :], NN)
        both[at, :] = done
        if kb < 3:
            below = slice(128 * kb + 128, 512)
            both[below, :] = both[below, :] - hdot(lead[below, at], done, NN)

    @pl.when(leads)
    def _():
        row_id = lax.broadcasted_iota(jnp.int32, (512, 512), 0)
        col_id = lax.broadcasted_iota(jnp.int32, (512, 512), 1)
        keep = jnp.logical_and(c == 0, col_id <= row_id)
        o_ref[...] = jnp.where(keep, lead[...], 0.0)

    @pl.when(jnp.logical_and(jnp.logical_not(leads), c == 0))
    def _():
        o_ref[...] = both[:, 0:512].T

    @pl.when(jnp.logical_and(jnp.logical_not(leads), c != 0))
    def _():
        o_ref[...] = tile[...] - hdot(both[:, 0:512], both[:, 512:1024], TN)

    @pl.when(r == 0)
    def _():
        for copy in fa_copies:
            copy.wait_send()

    @pl.when(root)
    def _():
        for copy in rs_copies[1:]:
            copy.wait_send()

    @pl.when(leads)
    def _():
        for copy in cs_copies[1:] + gs_copies[1:]:
            copy.wait_send()

        @pl.when(c != 0)
        def _():
            gs_copies[0].wait_send()

    @pl.when(c == 0)
    def _():
        for copy in rp_copies[1:]:
            copy.wait_send()

    for entry in u_copies + own_copies:
        @pl.when(jnp.logical_not(entry[0]))
        def _():
            entry[1].wait_send()

    for copy in fb_copies + d1_copies + [cpl_rem, inv_rem, inv_share]:
        copy.wait_send()
    for gather in (*ring_c, *ring_p, ring_g, spread_0, spread_f, spread_p):
        gather.drain()


def local(child_update, child_coupling, pivot_inverse, child_map, parent_front, block_pattern):
    vmem = pl.BlockSpec(memory_space=pltpu.VMEM)
    smem = pl.BlockSpec(memory_space=pltpu.SMEM)
    hbm = pl.BlockSpec(memory_space=pl.ANY)
    dma = pltpu.SemaphoreType.DMA

    def pair(n, m):
        return [dma((n,)), dma((m,))]

    return pl.pallas_call(
        kernel,
        out_shape=jax.ShapeDtypeStruct((512, 512), f32),
        in_specs=[smem, smem, hbm, hbm, hbm, hbm],
        out_specs=vmem,
        scratch_shapes=[
            pltpu.VMEM((2, 128, 2048), bf16),
            pltpu.VMEM((8, 2, 256, 128), bf16),
            pltpu.VMEM((256, 256), bf16),
            pltpu.VMEM((8, 2, 256, 256), bf16),
            pltpu.VMEM((16, 256, 256), bf16),
            pltpu.VMEM((2, 256, 256), f32),
            pltpu.VMEM((512, 512), f32),
            pltpu.VMEM((512, 512), f32),
            pltpu.VMEM((512, 512), bf16),
            pltpu.VMEM((16, 2, 32, 512), bf16),
            pltpu.VMEM((8, 64, 512), bf16),
            pltpu.VMEM((16, 32, 128), bf16),
            pltpu.VMEM((2, 8, 256, 256), bf16),
            pltpu.VMEM((2, 256, 256), f32),
            pltpu.VMEM((512, 512), f32),
            pltpu.VMEM((512, 1024), f32),
            pltpu.VMEM((128, 128), f32),
            pltpu.VMEM((4, 128, 128), f32),
            dma((3,)), *pair(8, 1), *pair(16, 16), *pair(16, 16), *pair(15, 15),
            *pair(2, 2), *pair(3, 3), *pair(2, 2), dma((2, 8)), dma((2, 8)), dma((2, 8)), dma((2, 8)),
            *pair(8, 8), *pair(2, 2), *pair(1, 1), *pair(16, 16), *pair(16, 16),
            *pair(16, 1), *pair(16, 1), *pair(16, 1), *pair(16, 1),
        ],
        compiler_params=pltpu.CompilerParams(
            has_side_effects=True, collective_id=0, vmem_limit_bytes=60 * 1024 * 1024
        ),
        cost_estimate=pl.CostEstimate(
            flops=8_000_000_000, bytes_accessed=4_000_000, transcendentals=512
        ),
    )(child_map, block_pattern, child_update, child_coupling, pivot_inverse, parent_front)


def solution(mesh):
    return jax.shard_map(
        local,
        mesh=mesh,
        in_specs=(
            P("sub", "row", "col"),
            P("sub", "row", "col"),
            P("sub", "col", None),
            P(),
            P(("sub", "row"), "col"),
            P(("sub", "row"), "col"),
        ),
        out_specs=P(("sub", "row"), "col"),
        check_vma=False,
    )
```
